256 devices in a mesh: dp: 8 (over z), tensor: 32 (over y, x, core).
Axes of the slice: x: 4, y: 4, z: 8, core: 2. Of those that a mesh axis runs over, the one named last changes fastest.
Arguments:
- activations: bfloat16 [4096, 4096], P('dp', 'tensor'), may hold values from -6 to 6
- cotangent: bfloat16 [4096, 4096], P('dp', 'tensor'), may hold values from -6 to 6
- gate_levels: bfloat16 [4096, 16384], P(None, 'tensor'), may hold values from -1 to 1
- up_levels: bfloat16 [4096, 16384], P(None, 'tensor'), may hold values from -1 to 1
- down_levels: bfloat16 [16384, 4096], P('tensor'), may hold values from -1 to 1
- gate_scales: int32 [64, 16384], P(None, 'tensor'), may hold values from 0 to 255
- up_scales: int32 [64, 16384], P(None, 'tensor'), may hold values from 0 to 255
- down_scales: int32 [256, 4096], P('tensor'), may hold values from 0 to 255
- scale_table: float32 [256], replicated, may hold values from 0.008 to 0.08
- block_pattern: int32 [32, 8, 3], P('tensor'), may hold values from 0 to 127, as said below
- delta_master: float32 [32, 8, 128, 128], P('tensor', 'dp'), may hold values from -0.12 to 0.12
- first_moment: bfloat16 [32, 8, 128, 128], P('tensor', 'dp'), may hold values from -12 to 12
- second_moment: bfloat16 [32, 8, 128, 128], P('tensor', 'dp'), may hold values from 0.049804688 to 5
Outputs:
- layer_output: bfloat16 [4096, 4096], P('dp', 'tensor')
- input_grad: bfloat16 [4096, 4096], P('dp', 'tensor')
- new_delta: float32 [32, 8, 128, 128], P('tensor', 'dp')
- new_first: bfloat16 [32, 8, 128, 128], P('tensor', 'dp')
- new_second: bfloat16 [32, 8, 128, 128], P('tensor', 'dp')
The draws below stay inside these ranges and needn't reach their ends.
Inputs may be any that keep to these rules, and one draw needn't show every extreme that they name: The blocks of block_pattern[t] are distinct; their hidden block index lies in t * (4) up to (t + 1) * 4 - 1, the width block index below 32, the projection in 0, 1, 2.
All inputs are finite; a program needn't handle non-finite values.
Results may differ from the reference program's by a relative error of at most 0.024.
Values may be sent and summed in bfloat16 or wider, within the bound.
A program may use at most 128 MiB of HBM per device.

```python
import math
import jax
import jax.numpy as jnp
from jax import lax

D = 4096
FF = 16384
BLK = 128
QBLK = 64
NSCALE = 256
ADAM_STEP = 20
TOKENS = 4096
SLOTS_T = 8
N_TENSOR = 32


def draw_block_pattern(key, part):
    key = jax.random.fold_in(key, 7)
    width_count = D // BLK
    shard_blocks = FF // BLK // N_TENSOR
    candidates = 3 * width_count * shard_blocks
    shard_keys = jax.random.split(key, N_TENSOR)

    def one_shard(shard_key, shard_index):
        noise_draw = jax.random.randint(shard_key, (candidates,), 0, 65536)
        forced_width = jax.random.randint(jax.random.fold_in(shard_key, 1), (), 0, width_count)
        positions = jnp.arange(candidates, dtype=jnp.int32)
        scores = noise_draw * candidates + positions
        forced = positions == forced_width * shard_blocks + shard_blocks - 1
        scores = jnp.where(forced, 65536 * candidates + positions, scores)
        _, picked = lax.top_k(scores, SLOTS_T)
        matrix = picked // (width_count * shard_blocks)
        remainder = picked % (width_count * shard_blocks)
        return jnp.stack([matrix, remainder // shard_blocks, shard_index * shard_blocks + remainder % shard_blocks], axis=1)
    return jax.vmap(one_shard)(shard_keys, jnp.arange(N_TENSOR, dtype=jnp.int32)).astype(jnp.int32)


def plant(values, stream_key, low, largest):
    dims = values.shape
    spot = [jax.random.randint(jax.random.fold_in(stream_key, axis), (), 0, dims[axis]) for axis in range(len(dims))]
    values = values.at[tuple(spot)].set(low)
    longest = dims.index(max(dims))
    spot[longest] = (spot[longest] + 1) % dims[longest]
    return values.at[tuple(spot)].set(largest)


def block_scale(key, extent, pieces, least, high):
    loudness, own = 1.0, jax.random.fold_in(key, 6)
    for dim, shards_of in pieces:
        steps = jnp.exp(jax.random.uniform(jax.random.fold_in(own, dim), (shards_of,), jnp.float32, least / len(pieces), high / len(pieces)))
        loudness = loudness * jnp.repeat(steps, extent[dim] // shards_of).reshape([-1 if axis == dim else 1 for axis in range(len(extent))])
    return loudness


def gaussian(stream_key, extent, spread, bound, cuts=(), kind=jnp.bfloat16):
    entries = spread * jax.random.normal(stream_key, extent, jnp.float32)
    if cuts:
        entries = entries * block_scale(stream_key, extent, cuts, -0.22, 0.18)
    return jnp.clip(entries, -bound, bound).astype(kind)


def setup_inputs(seed: int = 0) -> dict:
    key_of = jax.random.split(jax.random.key(seed), 14)
    return {
        "activations": gaussian(key_of[0], (TOKENS, D), 1.0, 6.0, ((0, 8), (1, 32))),
        "cotangent": gaussian(key_of[1], (TOKENS, D), 1.0, 6.0, ((0, 8), (1, 32))),
        "gate_levels": jnp.clip(jax.random.uniform(key_of[2], (D, FF), jnp.float32, -1.0, 1.0) * block_scale(key_of[2], (D, FF), ((1, 32),), -0.4, 0.0), -1.0, 1.0).astype(jnp.bfloat16),
        "up_levels": jnp.clip(jax.random.uniform(key_of[3], (D, FF), jnp.float32, -1.0, 1.0) * block_scale(key_of[3], (D, FF), ((1, 32),), -0.4, 0.0), -1.0, 1.0).astype(jnp.bfloat16),
        "down_levels": jnp.clip(jax.random.uniform(key_of[4], (FF, D), jnp.float32, -1.0, 1.0) * block_scale(key_of[4], (FF, D), ((0, 32),), -0.4, 0.0), -1.0, 1.0).astype(jnp.bfloat16),
        "gate_scales": plant(jax.random.randint(key_of[5], (D // QBLK, FF), 0, NSCALE), jax.random.fold_in(key_of[5], 1), 0, NSCALE - 1).astype(jnp.int32),
        "up_scales": plant(jax.random.randint(key_of[6], (D // QBLK, FF), 0, NSCALE), jax.random.fold_in(key_of[6], 1), 0, NSCALE - 1).astype(jnp.int32),
        "down_scales": plant(jax.random.randint(key_of[7], (FF // QBLK, D), 0, NSCALE), jax.random.fold_in(key_of[7], 1), 0, NSCALE - 1).astype(jnp.int32),
        "scale_table": jnp.clip(jnp.exp(jax.random.uniform(key_of[8], (NSCALE,), jnp.float32, math.log(0.008), math.log(0.08))), 0.008, 0.08),
        "block_pattern": draw_block_pattern(jax.random.fold_in(key_of[13], 71), 0),
        "delta_master": gaussian(key_of[10], (N_TENSOR, SLOTS_T, BLK, BLK), 0.02, 0.12, ((0, 32), (1, 8)), jnp.float32),
        "first_moment": gaussian(key_of[11], (N_TENSOR, SLOTS_T, BLK, BLK), 2.0, 12.0, ((0, 32), (1, 8))),
        "second_moment": jnp.clip(jnp.exp(math.log(5.0) - 4.609084 * jax.random.uniform(key_of[12], (N_TENSOR, SLOTS_T, BLK, BLK), jnp.float32) ** block_scale(key_of[12], (N_TENSOR, SLOTS_T, BLK, BLK), ((0, 32), (1, 8)), -0.2, 0.2)), 0.049804688, 5.0).astype(jnp.bfloat16),
    }


def expand(levels, scale_codes, scale_table):
    row_total, col_total = levels.shape
    scales = scale_table[scale_codes]
    grouped = levels.astype(jnp.float32).reshape(row_total // QBLK, QBLK, col_total) * scales[:, None, :]
    return grouped.reshape(row_total, col_total).astype(jnp.bfloat16)

def place(blocks, first_index, second_index, first_count, second_count):
    dense = jnp.zeros((first_count, second_count, BLK, BLK), jnp.float32)
    dense = dense.at[first_index, second_index].add(blocks)
    return dense.transpose(0, 2, 1, 3).reshape(first_count * BLK, second_count * BLK)

def pick_blocks(values, block_index):
    token_total = values.shape[0]
    return values.reshape(token_total, values.shape[1] // BLK, BLK)[:, block_index].astype(jnp.float32)

def reference(activations, cotangent, gate_levels, up_levels, down_levels, gate_scales, up_scales, down_scales, scale_table, block_pattern, delta_master, first_moment, second_moment):
    pattern = block_pattern.reshape(-1, 3)
    matrix = pattern[:, 0]
    width_block = pattern[:, 1]
    hidden_block = pattern[:, 2]
    used = delta_master.astype(jnp.bfloat16).astype(jnp.float32).reshape(-1, BLK, BLK)
    zero_blocks = jnp.zeros_like(used)
    width_count = D // BLK
    hidden_count = FF // BLK
    gate_add = place(jnp.where(matrix[:, None, None] == 0, used, zero_blocks), width_block, hidden_block, width_count, hidden_count)
    up_add = place(jnp.where(matrix[:, None, None] == 1, used, zero_blocks), width_block, hidden_block, width_count, hidden_count)
    down_add = place(jnp.where(matrix[:, None, None] == 2, used, zero_blocks), hidden_block, width_block, hidden_count, width_count)
    w_gate = (expand(gate_levels, gate_scales, scale_table).astype(jnp.float32) + gate_add).astype(jnp.bfloat16)
    w_up = (expand(up_levels, up_scales, scale_table).astype(jnp.float32) + up_add).astype(jnp.bfloat16)
    w_down = (expand(down_levels, down_scales, scale_table).astype(jnp.float32) + down_add).astype(jnp.bfloat16)
    gate_pre = jnp.dot(activations, w_gate, preferred_element_type=jnp.float32)
    up_pre = jnp.dot(activations, w_up, preferred_element_type=jnp.float32)
    sigmoid_gate = jax.nn.sigmoid(gate_pre)
    hidden = (gate_pre * sigmoid_gate * up_pre).astype(jnp.bfloat16)
    layer_output = jnp.dot(hidden, w_down, preferred_element_type=jnp.float32).astype(jnp.bfloat16)
    grad_hidden = jnp.dot(cotangent, w_down.T, preferred_element_type=jnp.float32)
    grad_up = (grad_hidden * gate_pre * sigmoid_gate).astype(jnp.bfloat16)
    grad_gate = (grad_hidden * up_pre * sigmoid_gate * (1.0 + gate_pre * (1.0 - sigmoid_gate))).astype(jnp.bfloat16)
    input_grad = (jnp.dot(grad_gate, w_gate.T, preferred_element_type=jnp.float32) + jnp.dot(grad_up, w_up.T, preferred_element_type=jnp.float32)).astype(jnp.bfloat16)
    x_blocks = pick_blocks(activations, width_block)
    dy_blocks = pick_blocks(cotangent, width_block)
    for_gate = jnp.einsum('tsa,tsb->sab', x_blocks, pick_blocks(grad_gate, hidden_block))
    for_up = jnp.einsum('tsa,tsb->sab', x_blocks, pick_blocks(grad_up, hidden_block))
    for_down = jnp.einsum('tsa,tsb->sab', pick_blocks(hidden, hidden_block), dy_blocks)
    selector = matrix[:, None, None]
    block_grad = jnp.where(selector == 0, for_gate, jnp.where(selector == 1, for_up, for_down)).reshape(delta_master.shape)
    moment = 0.9 * first_moment.astype(jnp.float32) + (1.0 - 0.9) * block_grad
    second = 0.999 * second_moment.astype(jnp.float32) + (1.0 - 0.999) * block_grad * block_grad
    bias_one = 1.0 - 0.9 ** ADAM_STEP
    bias_two = 1.0 - 0.999 ** ADAM_STEP
    step_size = 0.05 * (moment / bias_one) / (jnp.sqrt(second / bias_two) + 1e-08)
    new_delta = delta_master - step_size
    return (layer_output, input_grad, new_delta, moment.astype(jnp.bfloat16), second.astype(jnp.bfloat16))
```

```python
import jax
import jax.numpy as jnp
from jax import lax
from jax.experimental import pallas as pl
from jax.experimental.pallas import tpu as pltpu
from jax.sharding import PartitionSpec as P

BLK = 128
QBLK = 64
ADAM_STEP = 20


beta_one = 0.9
beta_two = 0.999
adam_eps = 1e-08
learn_rate = 0.05


def take_scales(codes, table_ref):
    low = jnp.broadcast_to(table_ref[0:1, :], codes.shape)
    high = jnp.broadcast_to(table_ref[1:2, :], codes.shape)
    within = jnp.bitwise_and(codes, 127)
    from_low = jnp.take_along_axis(low, within, axis=1, mode="promise_in_bounds")
    from_high = jnp.take_along_axis(high, within, axis=1, mode="promise_in_bounds")
    return jnp.where(codes < 128, from_low, from_high)


def scale_tile(levels, upper, lower, block):
    scales = jnp.concatenate(
        [jnp.broadcast_to(upper, (QBLK, BLK)), jnp.broadcast_to(lower, (QBLK, BLK))], axis=0
    )
    base = (levels.astype(jnp.float32) * scales).astype(jnp.bfloat16)
    return (base.astype(jnp.float32) + block.astype(jnp.float32)).astype(jnp.bfloat16)


def weights_kernel(
    gate_ref, up_ref, down_ref, gate_codes, up_codes, down_codes, table_ref, slot_of, blocks_ref,
    gate_out, up_out, down_out,
):
    width_count = gate_ref.shape[0] // BLK
    hidden_count = gate_ref.shape[1] // BLK

    for which, levels_ref, codes_ref, out_ref in (
        (0, gate_ref, gate_codes, gate_out), (1, up_ref, up_codes, up_out)
    ):
        @pl.loop(0, width_count // 4)
        def _(group):
            for hidden_at in range(hidden_count):
                lanes = pl.ds(hidden_at * BLK, BLK)
                codes = codes_ref[pl.ds(pl.multiple_of(group * 8, 8), 8), lanes]
                scales = take_scales(codes, table_ref)
                for inner in range(4):
                    at = group * 4 + inner
                    rows = pl.ds(pl.multiple_of(at * BLK, BLK), BLK)
                    slot = slot_of[(which * width_count + at) * hidden_count + hidden_at]
                    out_ref[rows, lanes] = scale_tile(
                        levels_ref[rows, lanes], scales[2 * inner : 2 * inner + 1],
                        scales[2 * inner + 1 : 2 * inner + 2], blocks_ref[slot],
                    )

    @pl.loop(0, width_count)
    def _(at):
        lanes = pl.ds(pl.multiple_of(at * BLK, BLK), BLK)
        scales = take_scales(down_codes[:, lanes], table_ref)
        for hidden_at in range(hidden_count):
            rows = pl.ds(hidden_at * BLK, BLK)
            slot = slot_of[(2 * width_count + at) * hidden_count + hidden_at]
            down_out[rows, lanes] = scale_tile(
                down_ref[rows, lanes], scales[2 * hidden_at : 2 * hidden_at + 1],
                scales[2 * hidden_at + 1 : 2 * hidden_at + 2], blocks_ref[slot],
            )


def slot_map(pattern, width_count, hidden_count, hidden_first):
    slots = pattern.shape[0]
    place = (pattern[:, 0] * width_count + pattern[:, 1]) * hidden_count + (
        pattern[:, 2] - hidden_first
    )
    tiles = jnp.arange(3 * width_count * hidden_count, dtype=jnp.int32)
    found = jnp.where(
        place[:, None] == tiles[None, :], jnp.arange(slots, dtype=jnp.int32)[:, None], slots
    )
    return jnp.min(found, axis=0)


def used_weights(
    gate_levels, up_levels, down_levels, gate_scales, up_scales, down_scales, scale_table,
    pattern, blocks,
):
    hidden_count = gate_levels.shape[1] // BLK
    slot_of = slot_map(
        pattern, gate_levels.shape[0] // BLK, hidden_count, lax.axis_index("tensor") * hidden_count
    )
    padded = jnp.concatenate([blocks, jnp.zeros((1, BLK, BLK), blocks.dtype)], axis=0)
    whole = pl.BlockSpec(memory_space=pltpu.VMEM)
    return pl.pallas_call(
        weights_kernel,
        out_shape=[jax.ShapeDtypeStruct(v.shape, v.dtype) for v in (gate_levels, up_levels, down_levels)],
        in_specs=[whole] * 7 + [pl.BlockSpec(memory_space=pltpu.SMEM), whole],
        out_specs=[whole] * 3,
        compiler_params=pltpu.CompilerParams(vmem_limit_bytes=48 * 1024 * 1024),
        cost_estimate=pl.CostEstimate(flops=12_000_000, bytes_accessed=30_000_000, transcendentals=0),
    )(
        gate_levels, up_levels, down_levels, gate_scales, up_scales, down_scales,
        scale_table.reshape(2, 128), slot_of, padded,
    )


def local(
    activations,
    cotangent,
    gate_levels,
    up_levels,
    down_levels,
    gate_scales,
    up_scales,
    down_scales,
    scale_table,
    block_pattern,
    delta_master,
    first_moment,
    second_moment,
):
    used_blocks = lax.all_gather(delta_master.astype(jnp.bfloat16), "dp", axis=1, tiled=True)
    pattern = block_pattern[0]
    blocks = used_blocks[0]
    ff_width = gate_levels.shape[1]
    ff_offset = lax.axis_index("tensor") * ff_width
    gate_w, up_w, down_w = used_weights(
        gate_levels, up_levels, down_levels, gate_scales, up_scales, down_scales, scale_table,
        pattern, blocks,
    )
    whole_x = lax.all_gather(activations, "tensor", axis=1, tiled=True)
    gate_pre = jnp.dot(whole_x, gate_w, preferred_element_type=jnp.float32)
    up_pre = jnp.dot(whole_x, up_w, preferred_element_type=jnp.float32)
    sigmoid_gate = jax.nn.sigmoid(gate_pre)
    hidden = (gate_pre * sigmoid_gate * up_pre).astype(jnp.bfloat16)
    contract_last = (((1,), (1,)), ((), ()))
    contract_first = (((0,), (0,)), ((), ()))
    whole_dy = lax.all_gather(cotangent, "tensor", axis=1, tiled=True)
    grad_hidden = lax.dot_general(
        whole_dy, down_w, contract_last, preferred_element_type=jnp.float32
    )
    grad_up = (grad_hidden * gate_pre * sigmoid_gate).astype(jnp.bfloat16)
    grad_gate = (
        grad_hidden * up_pre * sigmoid_gate * (1.0 + gate_pre * (1.0 - sigmoid_gate))
    ).astype(jnp.bfloat16)
    output_part = lax.psum_scatter(
        lax.dot_general(
            down_w, hidden, (((0,), (1,)), ((), ())), preferred_element_type=jnp.float32
        ).astype(jnp.bfloat16),
        "tensor",
        scatter_dimension=0,
        tiled=True,
    ).astype(jnp.float32)
    from_gate = lax.dot_general(
        gate_w, grad_gate, contract_last, preferred_element_type=jnp.float32
    )
    from_up = lax.dot_general(up_w, grad_up, contract_last, preferred_element_type=jnp.float32)
    input_part = lax.psum_scatter(
        (from_gate + from_up).astype(jnp.bfloat16), "tensor", scatter_dimension=0, tiled=True
    ).astype(jnp.float32)
    layer_output = output_part.T.astype(jnp.bfloat16)
    input_grad = input_part.T.astype(jnp.bfloat16)

    def slot_grad(slot_index, collected):
        matrix = pattern[slot_index, 0]
        width_at = pattern[slot_index, 1] * BLK
        hidden_at = pattern[slot_index, 2] * BLK - ff_offset
        x_part = lax.dynamic_slice_in_dim(whole_x, width_at, BLK, 1)
        dy_part = lax.dynamic_slice_in_dim(whole_dy, width_at, BLK, 1)
        gate_part = lax.dynamic_slice_in_dim(grad_gate, hidden_at, BLK, 1)
        up_part = lax.dynamic_slice_in_dim(grad_up, hidden_at, BLK, 1)
        hidden_part = lax.dynamic_slice_in_dim(hidden, hidden_at, BLK, 1)
        for_gate = lax.dot_general(
            x_part, gate_part, contract_first, preferred_element_type=jnp.float32
        )
        for_up = lax.dot_general(
            x_part, up_part, contract_first, preferred_element_type=jnp.float32
        )
        for_down = lax.dot_general(
            hidden_part, dy_part, contract_first, preferred_element_type=jnp.float32
        )
        chosen = jnp.where(matrix == 0, for_gate, jnp.where(matrix == 1, for_up, for_down))
        return lax.dynamic_update_slice(collected, chosen[None], (slot_index, 0, 0))

    slot_total = pattern.shape[0]
    block_grads = lax.fori_loop(
        0, slot_total, slot_grad, jnp.zeros((slot_total, BLK, BLK), jnp.float32)
    )[None]
    owned = delta_master.shape[1]
    total_grads = lax.psum(block_grads.astype(jnp.bfloat16), "dp").astype(jnp.float32)
    own_grads = lax.dynamic_slice_in_dim(total_grads, lax.axis_index("dp") * owned, owned, 1)
    moment = beta_one * first_moment.astype(jnp.float32) + (1.0 - beta_one) * own_grads
    second = beta_two * second_moment.astype(jnp.float32) + (1.0 - beta_two) * own_grads * own_grads
    bias_one = 1.0 - beta_one**ADAM_STEP
    bias_two = 1.0 - beta_two**ADAM_STEP
    step_size = learn_rate * (moment / bias_one) / (jnp.sqrt(second / bias_two) + adam_eps)
    new_delta = delta_master - step_size
    return (
        layer_output,
        input_grad,
        new_delta,
        moment.astype(jnp.bfloat16),
        second.astype(jnp.bfloat16),
    )


def solution(mesh):
    in_specs = (
        P("dp", "tensor"),
        P("dp", "tensor"),
        P(None, "tensor"),
        P(None, "tensor"),
        P("tensor", None),
        P(None, "tensor"),
        P(None, "tensor"),
        P("tensor", None),
        P(),
        P("tensor", None, None),
        P("tensor", "dp", None, None),
        P("tensor", "dp", None, None),
        P("tensor", "dp", None, None),
    )
    out_specs = (
        P("dp", "tensor"),
        P("dp", "tensor"),
        P("tensor", "dp", None, None),
        P("tensor", "dp", None, None),
        P("tensor", "dp", None, None),
    )
    return jax.shard_map(local, mesh=mesh, in_specs=in_specs, out_specs=out_specs, check_vma=False)
```

```python
import functools

import jax
import jax.numpy as jnp
from jax import lax
from jax.experimental import pallas as pl
from jax.experimental.pallas import tpu as pltpu
from jax.sharding import PartitionSpec as P

BLK = 128
QBLK = 64
ADAM_STEP = 20
SIDE = 4
CORES = 2
SEMAPHORES = 256

beta_one = 0.9
beta_two = 0.999
adam_eps = 1e-08
learn_rate = 0.05

MESH = pl.DeviceIdType.MESH
contract_last = (((1,), (1,)), ((), ()))
contract_first = (((0,), (0,)), ((), ()))


def take_scales(codes, table_ref):
    low = jnp.broadcast_to(table_ref[0:1, :], codes.shape)
    high = jnp.broadcast_to(table_ref[1:2, :], codes.shape)
    within = jnp.bitwise_and(codes, 127)
    from_low = jnp.take_along_axis(low, within, axis=1, mode="promise_in_bounds")
    from_high = jnp.take_along_axis(high, within, axis=1, mode="promise_in_bounds")
    return jnp.where(codes < 128, from_low, from_high)


def scale_tile(levels, upper, lower, block):
    scales = jnp.concatenate(
        [jnp.broadcast_to(upper, (QBLK, BLK)), jnp.broadcast_to(lower, (QBLK, BLK))], axis=0
    )
    base = (levels.astype(jnp.float32) * scales).astype(jnp.bfloat16)
    return (base.astype(jnp.float32) + block.astype(jnp.float32)).astype(jnp.bfloat16)


def layer_kernel(
    groups,
    x_ref, dy_ref, gate_levels, up_levels, down_levels, gate_codes, up_codes, down_codes, table_ref,
    picks, delta_ref, first_ref, second_ref,
    out_ref, input_ref, new_delta, new_first, new_second,
    held, gate_w, up_w, down_w, gate_pre, up_pre, grad_hidden, deltas,
    out_parts, input_parts, out_pair, input_pair, far_one, far_all, near_one, near_all,
    grads, grads_in, send_sem, recv_sem, load_sem,
):
    tokens = x_ref.shape[0]
    hidden_count = gate_w.shape[1] // BLK
    width_count = gate_w.shape[0] // BLK
    tensor = width_count
    half, part = tokens // 2, tokens // 4
    z, t = lax.axis_index("dp"), lax.axis_index("tensor")
    core = lax.rem(t, CORES)
    x = lax.rem(lax.div(t, CORES), SIDE)
    y = lax.div(t, CORES * SIDE)

    def spot(dy, dx, which=None):
        row, col = lax.rem(y + dy, SIDE), lax.rem(x + dx, SIDE)
        return (row * SIDE + col) * CORES + (core if which is None else which)

    other = 1 - core
    sibling = spot(0, 0, other)

    indices, sends = {}, []

    def recv_at(key):
        return indices.setdefault(key, len(indices))

    def push(src, dst, to, key):
        copy = pltpu.make_async_remote_copy(
            src_ref=src, dst_ref=dst, send_sem=send_sem.at[len(sends)],
            recv_sem=recv_sem.at[recv_at(key)], device_id=to, device_id_type=MESH,
        )
        copy.start()
        sends.append(copy)

    def arrived(dst, key):
        pltpu.make_async_remote_copy(
            src_ref=dst, dst_ref=dst, send_sem=send_sem.at[0], recv_sem=recv_sem.at[recv_at(key)],
            device_id=(z, sibling), device_id_type=MESH,
        ).wait_recv()

    loads = [
        pltpu.make_async_copy(src, dst, load_sem.at[at])
        for at, (src, dst) in enumerate(
            ((gate_levels, gate_w), (up_levels, up_w), (down_levels, down_w))
        )
    ]
    for load in loads:
        load.start()
    barrier = pltpu.get_barrier_semaphore()
    partners = [(z, spot(0, 1)), (z, spot(0, 3)), (z, spot(1, 0)), (z, spot(3, 0)), (z, sibling)]
    partners += [(lax.rem(z + step, groups), t) for step in range(1, groups)]
    for partner in partners:
        pl.semaphore_signal(barrier, inc=1, device_id=partner, device_id_type=MESH)
    held[t] = x_ref[...]
    held[tensor + t] = dy_ref[...]
    deltas[z] = delta_ref[0, 0].astype(jnp.bfloat16)
    deltas[groups] = jnp.zeros((BLK, BLK), jnp.bfloat16)
    pl.semaphore_wait(barrier, len(partners))

    def block(g, h, dp, ds, piece=None, which=None):
        at = spot(ds, dp, which) if h == 0 else spot(dp, ds, which)
        rows = pl.ds(h * half, half) if piece is None else pl.ds(h * half + piece * part, part)
        return held.at[g * tensor + at, rows]

    def node(h, dp, ds):
        return (z, spot(ds, dp) if h == 0 else spot(dp, ds))

    def spread(g, h, dp):
        whole = block(g, h, dp, 0)
        push(whole, whole, node(h, 0, 1), ("g", g, h, dp, 3, 0))
        push(whole, whole, node(h, 0, 3), ("g", g, h, dp, 1, 0))
        push(whole, whole, (z, sibling), ("s", g, h, dp, 0))

    def gather_zero(g):
        for h in range(2):
            whole = block(g, h, 0, 0)
            push(whole, whole, node(h, 1, 0), ("g", g, h, 3, 0, 0))
            push(whole, whole, node(h, 3, 0), ("g", g, h, 1, 0, 0))
        for h in range(2):
            spread(g, h, 0)

    def gather_one(g):
        for h in range(2):
            for dp, piece, onward in ((3, 0, 1), (1, 1, 3)):
                arrived(block(g, h, dp, 0), ("g", g, h, dp, 0, 0))
                quarter = block(g, h, dp, 0, piece)
                push(quarter, quarter, node(h, onward, 0), ("g", g, h, 2, 0, piece))
        for h in range(2):
            for dp in (3, 1):
                spread(g, h, dp)

    def gather_two(g):
        for h in range(2):
            for piece in range(2):
                arrived(block(g, h, 2, 0, piece), ("g", g, h, 2, 0, piece))
            spread(g, h, 2)

    def gather_three(g, dp):
        for h in range(2):
            for ds, piece, onward in ((3, 0, 1), (1, 1, 3)):
                whole, quarter = block(g, h, dp, ds), block(g, h, dp, ds, piece)
                arrived(whole, ("g", g, h, dp, ds, 0))
                push(quarter, quarter, node(h, 0, onward), ("g", g, h, dp, 2, piece))
                push(whole, whole, (z, sibling), ("s", g, h, dp, ds))

    def gather_four(g, dp):
        for h in range(2):
            for piece in range(2):
                arrived(block(g, h, dp, 2, piece), ("g", g, h, dp, 2, piece))
            whole = block(g, h, dp, 2)
            push(whole, whole, (z, sibling), ("s", g, h, dp, 2))

    def gather_five(g):
        for h in range(2):
            for dp in range(SIDE):
                for ds in range(SIDE):
                    arrived(block(g, h, dp, ds, None, other), ("s", g, h, dp, ds))

    def wide_weights(which, weight, codes_ref, first_group, last_group):
        @pl.loop(first_group, last_group)
        def _(group):
            for hidden_at in range(hidden_count):
                lanes = pl.ds(hidden_at * BLK, BLK)
                codes = codes_ref[pl.ds(pl.multiple_of(group * 8, 8), 8), lanes]
                scales = take_scales(codes, table_ref)
                for inner in range(4):
                    at = group * 4 + inner
                    rows = pl.ds(pl.multiple_of(at * BLK, BLK), BLK)
                    slot = picks[(which * width_count + at) * hidden_count + hidden_at]
                    weight[rows, lanes] = scale_tile(
                        weight[rows, lanes], scales[2 * inner : 2 * inner + 1],
                        scales[2 * inner + 1 : 2 * inner + 2], deltas[slot],
                    )

    def down_weights(first_at, last_at):
        @pl.loop(first_at, last_at)
        def _(at):
            lanes = pl.ds(pl.multiple_of(at * BLK, BLK), BLK)
            scales = take_scales(down_codes[:, lanes], table_ref)
            for hidden_at in range(hidden_count):
                rows = pl.ds(hidden_at * BLK, BLK)
                slot = picks[(2 * width_count + at) * hidden_count + hidden_at]
                down_w[rows, lanes] = scale_tile(
                    down_w[rows, lanes], scales[2 * hidden_at : 2 * hidden_at + 1],
                    scales[2 * hidden_at + 1 : 2 * hidden_at + 2], deltas[slot],
                )

    def across(first, count):
        return jnp.concatenate([held[first + at] for at in range(count)], axis=1)

    def project(weight, into):
        into[...] = jnp.zeros_like(into)

        @pl.loop(0, width_count // 8)
        def _(step):
            rows = pl.ds(pl.multiple_of(step * 8 * BLK, BLK), 8 * BLK)
            into[...] += jnp.dot(
                across(step * 8, 8), weight[rows, :], preferred_element_type=jnp.float32
            )

    def activate():
        @pl.loop(0, tokens // BLK)
        def _(chunk):
            rows = pl.ds(pl.multiple_of(chunk * BLK, BLK), BLK)
            for at in range(hidden_count):
                lanes = pl.ds(at * BLK, BLK)
                gate, up = gate_pre[rows, lanes], up_pre[rows, lanes]
                sig = 1.0 / (1.0 + jnp.exp(-gate))
                gated = gate * sig
                held[2 * tensor + at, rows] = (gated * up).astype(jnp.bfloat16)
                gate_pre[rows, lanes] = gated
                up_pre[rows, lanes] = up * sig * (1.0 + gate * (1.0 - sig))

    def back_hidden():
        grad_hidden[...] = jnp.zeros_like(grad_hidden)

        @pl.loop(0, width_count // 8)
        def _(step):
            lanes = pl.ds(pl.multiple_of(step * 8 * BLK, BLK), 8 * BLK)
            grad_hidden[...] += lax.dot_general(
                across(tensor + step * 8, 8), down_w[:, lanes], contract_last,
                preferred_element_type=jnp.float32,
            )

        @pl.loop(0, tokens // BLK)
        def _(chunk):
            rows = pl.ds(pl.multiple_of(chunk * BLK, BLK), BLK)
            for at in range(hidden_count):
                lanes = pl.ds(at * BLK, BLK)
                grad = grad_hidden[rows, lanes]
                held[2 * tensor + hidden_count + at, rows] = (grad * up_pre[rows, lanes]).astype(
                    jnp.bfloat16
                )
                held[2 * tensor + 2 * hidden_count + at, rows] = (
                    grad * gate_pre[rows, lanes]
                ).astype(jnp.bfloat16)

    parts, pairs = (out_parts, input_parts), (out_pair, input_pair)

    def share(r, row, col):
        chip = row * SIDE + col
        if r == 0:
            columns = pl.ds(pl.multiple_of(chip * 2 * BLK, 2 * BLK), 2 * BLK)
            return jnp.dot(
                across(2 * tensor, hidden_count), down_w[:, columns],
                preferred_element_type=jnp.float32,
            )
        rows = pl.ds(pl.multiple_of(chip * 2 * BLK, 2 * BLK), 2 * BLK)
        return lax.dot_general(
            across(2 * tensor + hidden_count, hidden_count), gate_w[rows, :], contract_last,
            preferred_element_type=jnp.float32,
        ) + lax.dot_general(
            across(2 * tensor + 2 * hidden_count, hidden_count), up_w[rows, :], contract_last,
            preferred_element_type=jnp.float32,
        )

    def pair_copy(r, row, col, sends_at, recvs_at):
        return pltpu.make_async_remote_copy(
            src_ref=parts[r].at[row, col, other], dst_ref=pairs[r].at[row, col],
            send_sem=send_sem.at[sends_at], recv_sem=recv_sem.at[recvs_at],
            device_id=(z, sibling), device_id_type=MESH,
        )

    pair_at = {}

    def make_parts(r, dy):
        sends_at, recvs_at = len(sends), len(indices)
        row = lax.rem(y + dy, SIDE)
        pair_at[r, dy] = (sends_at, recvs_at)
        for col in range(SIDE):
            recv_at(("p", r, dy, col))
            sends.append(pair_copy(r, row, col, sends_at + col, recvs_at + col))

        @pl.loop(0, SIDE)
        def _(col):
            both = share(r, row, col).astype(jnp.bfloat16)
            parts[r][row, col, 0] = both[:, :BLK]
            parts[r][row, col, 1] = both[:, BLK:]
            pair_copy(r, row, col, sends_at + col, recvs_at + col).start()

    def add_pairs(r, dy):
        sends_at, recvs_at = pair_at[r, dy]
        row = lax.rem(y + dy, SIDE)

        @pl.loop(0, SIDE)
        def _(col):
            pair_copy(r, row, col, sends_at + col, recvs_at + col).wait_recv()
            parts[r][row, col, core] = (
                parts[r][row, col, core].astype(jnp.float32)
                + pairs[r][row, col].astype(jnp.float32)
            ).astype(jnp.bfloat16)

    def line(r, h, df, rows):
        if h == 0:
            return parts[r].at[lax.rem(y + df, SIDE), :, core, rows]
        return parts[r].at[:, lax.rem(x + df, SIDE), core, rows]

    def cell(r, h, dg, rows):
        if h == 0:
            return parts[r].at[y, lax.rem(x + dg, SIDE), core, rows]
        return parts[r].at[lax.rem(y + dg, SIDE), x, core, rows]

    def far(h, df):
        return (z, spot(df, 0) if h == 0 else spot(0, df))

    def near(h, dg):
        return (z, spot(0, dg) if h == 0 else spot(dg, 0))

    def whole_rows(h):
        return pl.ds(h * half, half)

    def part_rows(h, piece):
        return pl.ds(h * half + piece * part, part)

    ways = ((0, 1), (1, 3))

    def reduce_one(r, h):
        for piece, onward in ways:
            push(line(r, h, 2, part_rows(h, piece)), far_one.at[r, h, piece], far(h, onward), ("a", r, h, piece))

    def reduce_two(r, h):
        for piece, onward in ways:
            arrived(far_one.at[r, h, piece], ("a", r, h, piece))
            target = line(r, h, onward, part_rows(h, piece))

            @pl.loop(0, SIDE)
            def _(at):
                target[at] = (
                    target[at].astype(jnp.float32) + far_one[r, h, piece, at].astype(jnp.float32)
                ).astype(jnp.bfloat16)

            push(line(r, h, onward, whole_rows(h)), far_all.at[r, h, piece], far(h, onward), ("b", r, h, piece))

    def reduce_three(r, h):
        for piece in range(2):
            arrived(far_all.at[r, h, piece], ("b", r, h, piece))
        target = line(r, h, 0, whole_rows(h))

        @pl.loop(0, SIDE)
        def _(at):
            target[at] = (
                target[at].astype(jnp.float32)
                + far_all[r, h, 0, at].astype(jnp.float32)
                + far_all[r, h, 1, at].astype(jnp.float32)
            ).astype(jnp.bfloat16)

        for piece, onward in ways:
            push(cell(r, h, 2, part_rows(h, piece)), near_one.at[r, h, piece], near(h, onward), ("c", r, h, piece))

    def reduce_four(r, h):
        for piece, onward in ways:
            arrived(near_one.at[r, h, piece], ("c", r, h, piece))
            target = cell(r, h, onward, part_rows(h, piece))
            target[...] = (
                target[...].astype(jnp.float32) + near_one[r, h, piece].astype(jnp.float32)
            ).astype(jnp.bfloat16)
            push(cell(r, h, onward, whole_rows(h)), near_all.at[r, h, piece], near(h, onward), ("d", r, h, piece))

    def reduce_five(r, h, result):
        for piece in range(2):
            arrived(near_all.at[r, h, piece], ("d", r, h, piece))
        result[pl.ds(h * half, half), :] = (
            cell(r, h, 0, whole_rows(h))[...].astype(jnp.float32)
            + near_all[r, h, 0].astype(jnp.float32)
            + near_all[r, h, 1].astype(jnp.float32)
        ).astype(jnp.bfloat16)

    def block_grads():
        base = 3 * width_count * hidden_count

        @pl.loop(0, groups)
        def _(slot):
            grads[slot] = lax.dot_general(
                held[picks[base + slot]], held[picks[base + groups + slot]], contract_first,
                preferred_element_type=jnp.float32,
            ).astype(jnp.bfloat16)

        for step in range(1, groups):
            to = lax.rem(z + step, groups)
            push(grads.at[to], grads_in.at[step - 1], (to, t), ("h", step))

    def adam():
        total = grads[z].astype(jnp.float32)
        for step in range(1, groups):
            arrived(grads_in.at[step - 1], ("h", step))
            total = total + grads_in[step - 1].astype(jnp.float32)
        moment = beta_one * first_ref[0, 0].astype(jnp.float32) + (1.0 - beta_one) * total
        second = (
            beta_two * second_ref[0, 0].astype(jnp.float32) + (1.0 - beta_two) * total * total
        )
        bias_one = 1.0 - beta_one**ADAM_STEP
        bias_two = 1.0 - beta_two**ADAM_STEP
        step_size = learn_rate * (moment / bias_one) / (jnp.sqrt(second / bias_two) + adam_eps)
        new_delta[0, 0] = delta_ref[0, 0] - step_size
        new_first[0, 0] = moment.astype(jnp.bfloat16)
        new_second[0, 0] = second.astype(jnp.bfloat16)

    gather_zero(0)
    for step in range(1, groups):
        push(deltas.at[z], deltas.at[z], (lax.rem(z + step, groups), t), ("w", step))
    for load in loads:
        load.wait()
    gather_one(0)
    for step in range(1, groups):
        arrived(deltas.at[lax.rem(z + groups - step, groups)], ("w", step))
    wide_weights(0, gate_w, gate_codes, 0, 4)
    gather_two(0)
    gather_three(0, 0)
    wide_weights(0, gate_w, gate_codes, 4, 8)
    gather_three(0, 3)
    gather_three(0, 1)
    gather_zero(1)
    wide_weights(1, up_w, up_codes, 0, 4)
    gather_three(0, 2)
    gather_four(0, 0)
    wide_weights(1, up_w, up_codes, 4, 8)
    for dp in (3, 1, 2):
        gather_four(0, dp)
    gather_one(1)
    gather_five(0)
    project(gate_w, gate_pre)
    gather_two(1)
    gather_three(1, 0)
    project(up_w, up_pre)
    gather_three(1, 3)
    gather_three(1, 1)
    activate()
    gather_three(1, 2)
    gather_four(1, 0)
    down_weights(0, width_count)
    for dp in (3, 1, 2):
        gather_four(1, dp)
    for dy in (2, 1, 3, 0):
        make_parts(0, dy)
    add_pairs(0, 2)
    reduce_one(0, 0)
    for dy in (1, 3, 0):
        add_pairs(0, dy)
    reduce_one(0, 1)
    gather_five(1)
    back_hidden()
    for h in range(2):
        reduce_two(0, h)
    make_parts(1, 2)
    make_parts(1, 1)
    for h in range(2):
        reduce_three(0, h)
    make_parts(1, 3)
    make_parts(1, 0)
    for h in range(2):
        reduce_four(0, h)
    add_pairs(1, 2)
    reduce_one(1, 0)
    for dy in (1, 3, 0):
        add_pairs(1, dy)
    reduce_one(1, 1)
    block_grads()
    for h in range(2):
        reduce_five(0, h, out_ref)
    for h in range(2):
        reduce_two(1, h)
    adam()
    for h in range(2):
        reduce_three(1, h)
    for h in range(2):
        reduce_four(1, h)
    for h in range(2):
        reduce_five(1, h, input_ref)
    for copy in sends:
        copy.wait_send()
    assert len(sends) <= SEMAPHORES and len(indices) <= SEMAPHORES


def slot_picks(pattern, width_count, hidden_count, hidden_first):
    slots = pattern.shape[0]
    matrix, width_at, hidden_at = pattern[:, 0], pattern[:, 1], pattern[:, 2] - hidden_first
    place = (matrix * width_count + width_at) * hidden_count + hidden_at
    tiles = jnp.arange(3 * width_count * hidden_count, dtype=jnp.int32)
    found = jnp.where(
        place[:, None] == tiles[None, :], jnp.arange(slots, dtype=jnp.int32)[:, None], slots
    )
    base = 2 * width_count
    left = jnp.where(matrix == 2, base + hidden_at, width_at)
    right = jnp.where(
        matrix == 2, width_count + width_at, base + (1 + matrix) * hidden_count + hidden_at
    )
    return jnp.concatenate([jnp.min(found, axis=0), left, right])


def local(
    groups,
    activations, cotangent, gate_levels, up_levels, down_levels, gate_scales, up_scales, down_scales,
    scale_table, block_pattern, delta_master, first_moment, second_moment,
):
    tokens = activations.shape[0]
    width, hidden = gate_levels.shape
    width_count, hidden_count = width // BLK, hidden // BLK
    half, part = tokens // 2, tokens // 4
    picks = slot_picks(
        block_pattern[0], width_count, hidden_count, lax.axis_index("tensor") * hidden_count
    )
    vmem = pl.BlockSpec(memory_space=pltpu.VMEM)
    anywhere = pl.BlockSpec(memory_space=pl.ANY)
    narrow, wide = jnp.bfloat16, jnp.float32
    return pl.pallas_call(
        functools.partial(layer_kernel, groups),
        out_shape=[
            jax.ShapeDtypeStruct(v.shape, v.dtype)
            for v in (activations, activations, delta_master, first_moment, second_moment)
        ],
        in_specs=[vmem, vmem, anywhere, anywhere, anywhere, vmem, vmem, vmem, vmem]
        + [pl.BlockSpec(memory_space=pltpu.SMEM), vmem, vmem, vmem],
        out_specs=[vmem] * 5,
        scratch_shapes=[
            pltpu.VMEM((2 * width_count + 3 * hidden_count, tokens, BLK), narrow),
            pltpu.VMEM((width, hidden), narrow),
            pltpu.VMEM((width, hidden), narrow),
            pltpu.VMEM((hidden, width), narrow),
            pltpu.VMEM((tokens, hidden), wide),
            pltpu.VMEM((tokens, hidden), wide),
            pltpu.VMEM((tokens, hidden), wide),
            pltpu.VMEM((groups + 1, BLK, BLK), narrow),
            pltpu.VMEM((SIDE, SIDE, CORES, tokens, BLK), narrow),
            pltpu.VMEM((SIDE, SIDE, CORES, tokens, BLK), narrow),
            pltpu.VMEM((SIDE, SIDE, tokens, BLK), narrow),
            pltpu.VMEM((SIDE, SIDE, tokens, BLK), narrow),
            pltpu.VMEM((2, 2, 2, SIDE, part, BLK), narrow),
            pltpu.VMEM((2, 2, 2, SIDE, half, BLK), narrow),
            pltpu.VMEM((2, 2, 2, part, BLK), narrow),
            pltpu.VMEM((2, 2, 2, half, BLK), narrow),
            pltpu.VMEM((groups, BLK, BLK), narrow),
            pltpu.VMEM((groups - 1, BLK, BLK), narrow),
            pltpu.SemaphoreType.DMA((SEMAPHORES,)),
            pltpu.SemaphoreType.DMA((SEMAPHORES,)),
            pltpu.SemaphoreType.DMA((3,)),
        ],
        compiler_params=pltpu.CompilerParams(
            collective_id=0, has_side_effects=True, vmem_limit_bytes=58 * 1024 * 1024
        ),
        cost_estimate=pl.CostEstimate(
            flops=13_000_000_000, bytes_accessed=14_000_000, transcendentals=262_144
        ),
    )(
        activations, cotangent, gate_levels, up_levels, down_levels, gate_scales, up_scales,
        down_scales, scale_table.reshape(2, 128), picks, delta_master, first_moment, second_moment,
    )


def solution(mesh):
    in_specs = (
        P("dp", "tensor"),
        P("dp", "tensor"),
        P(None, "tensor"),
        P(None, "tensor"),
        P("tensor", None),
        P(None, "tensor"),
        P(None, "tensor"),
        P("tensor", None),
        P(),
        P("tensor", None, None),
        P("tensor", "dp", None, None),
        P("tensor", "dp", None, None),
        P("tensor", "dp", None, None),
    )
    out_specs = (
        P("dp", "tensor"),
        P("dp", "tensor"),
        P("tensor", "dp", None, None),
        P("tensor", "dp", None, None),
        P("tensor", "dp", None, None),
    )
    return jax.shard_map(
        functools.partial(local, mesh.shape["dp"]),
        mesh=mesh, in_specs=in_specs, out_specs=out_specs, check_vma=False,
    )
```

```python
import functools

import jax
import jax.numpy as jnp
from jax import lax
from jax.experimental import pallas as pl
from jax.experimental.pallas import tpu as pltpu
from jax.sharding import PartitionSpec as P

BLK = 128
QBLK = 64
ADAM_STEP = 20
SIDE = 4
CORES = 2
SEMAPHORES = 288

beta_one = 0.9
beta_two = 0.999
adam_eps = 1e-08
learn_rate = 0.05

MESH = pl.DeviceIdType.MESH
contract_last = (((1,), (1,)), ((), ()))
contract_first = (((0,), (0,)), ((), ()))


def take_scales(codes, table_ref):
    low = jnp.broadcast_to(table_ref[0:1, 0:128], codes.shape)
    high = jnp.broadcast_to(table_ref[0:1, 128:256], codes.shape)
    within = jnp.bitwise_and(codes, 127)
    from_low = jnp.take_along_axis(low, within, axis=1, mode="promise_in_bounds")
    from_high = jnp.take_along_axis(high, within, axis=1, mode="promise_in_bounds")
    return jnp.where(codes < 128, from_low, from_high)


def scale_tile(levels, upper, lower, block):
    scales = jnp.concatenate(
        [jnp.broadcast_to(upper, (QBLK, BLK)), jnp.broadcast_to(lower, (QBLK, BLK))], axis=0
    )
    base = (levels.astype(jnp.float32) * scales).astype(jnp.bfloat16)
    return (base.astype(jnp.float32) + block.astype(jnp.float32)).astype(jnp.bfloat16)


def layer_kernel(
    groups,
    x_ref, dy_ref, gate_levels, up_levels, down_levels, gate_scales, up_scales, down_scales, table_ref,
    picks, delta_ref, first_ref, second_ref,
    out_ref, input_ref, new_delta, new_first, new_second,
    held, gate_w, up_w, down_w, gate_codes, up_codes, down_codes, gate_pre, up_pre, grad_hidden, deltas,
    out_parts, input_parts, out_pair, input_pair, far_one, far_all, near_one, near_all,
    grads, grads_in, send_sem, recv_sem, pair_send, pair_recv, load_sem,
):
    tokens = x_ref.shape[0]
    hidden_count = gate_w.shape[1] // BLK
    width_count = gate_w.shape[0] // BLK
    tensor = width_count
    half, part = tokens // 2, tokens // 4
    z, t = lax.axis_index("dp"), lax.axis_index("tensor")
    core = lax.rem(t, CORES)
    x = lax.rem(lax.div(t, CORES), SIDE)
    y = lax.div(t, CORES * SIDE)

    def spot(dy, dx, which=None):
        row, col = lax.rem(y + dy, SIDE), lax.rem(x + dx, SIDE)
        return (row * SIDE + col) * CORES + (core if which is None else which)

    other = 1 - core
    sibling = spot(0, 0, other)

    indices, sends = {}, []

    def recv_at(key):
        return indices.setdefault(key, len(indices))

    def push(src, dst, to, key):
        copy = pltpu.make_async_remote_copy(
            src_ref=src, dst_ref=dst, send_sem=send_sem.at[len(sends)],
            recv_sem=recv_sem.at[recv_at(key)], device_id=to, device_id_type=MESH,
        )
        copy.start()
        sends.append(copy)

    def arrived(dst, key):
        pltpu.make_async_remote_copy(
            src_ref=dst, dst_ref=dst, send_sem=send_sem.at[0], recv_sem=recv_sem.at[recv_at(key)],
            device_id=(z, sibling), device_id_type=MESH,
        ).wait_recv()

    loads = [
        pltpu.make_async_copy(src, dst, load_sem.at[at])
        for at, (src, dst) in enumerate(
            (
                (x_ref, held.at[t]), (dy_ref, held.at[tensor + t]),
                (gate_scales, gate_codes), (gate_levels, gate_w),
                (up_scales, up_codes), (up_levels, up_w),
                (down_scales, down_codes), (down_levels, down_w),
            )
        )
    ]
    for load in loads:
        load.start()
    barrier = pltpu.get_barrier_semaphore()
    partners = [(z, spot(0, 1)), (z, spot(0, 3)), (z, spot(1, 0)), (z, spot(3, 0)), (z, sibling)]
    partners += [(lax.rem(z + step, groups), t) for step in range(1, groups)]
    for partner in partners:
        pl.semaphore_signal(barrier, inc=1, device_id=partner, device_id_type=MESH)
    deltas[z] = delta_ref[0, 0].astype(jnp.bfloat16)
    deltas[groups] = jnp.zeros((BLK, BLK), jnp.bfloat16)
    loads[0].wait()
    pl.semaphore_wait(barrier, len(partners))

    def block(g, h, dp, ds, piece=None, which=None):
        at = spot(ds, dp, which) if h == 0 else spot(dp, ds, which)
        rows = pl.ds(h * half, half) if piece is None else pl.ds(h * half + piece * part, part)
        return held.at[g * tensor + at, rows]

    def node(h, dp, ds):
        return (z, spot(ds, dp) if h == 0 else spot(dp, ds))

    def spread(g, h, dp):
        whole = block(g, h, dp, 0)
        push(whole, whole, node(h, 0, 1), ("g", g, h, dp, 3, 0))
        push(whole, whole, node(h, 0, 3), ("g", g, h, dp, 1, 0))
        push(whole, whole, (z, sibling), ("s", g, h, dp, 0))

    def gather_zero(g):
        for h in range(2):
            whole = block(g, h, 0, 0)
            push(whole, whole, node(h, 1, 0), ("g", g, h, 3, 0, 0))
            push(whole, whole, node(h, 3, 0), ("g", g, h, 1, 0, 0))
        for h in range(2):
            spread(g, h, 0)

    def gather_one(g):
        for h in range(2):
            for dp, piece, onward in ((3, 0, 1), (1, 1, 3)):
                arrived(block(g, h, dp, 0), ("g", g, h, dp, 0, 0))
                quarter = block(g, h, dp, 0, piece)
                push(quarter, quarter, node(h, onward, 0), ("g", g, h, 2, 0, piece))
        for h in range(2):
            for dp in (3, 1):
                spread(g, h, dp)

    def gather_two(g):
        for h in range(2):
            for piece in range(2):
                arrived(block(g, h, 2, 0, piece), ("g", g, h, 2, 0, piece))
            spread(g, h, 2)

    def gather_three(g, dp):
        for h in range(2):
            for ds, piece, onward in ((3, 0, 1), (1, 1, 3)):
                whole, quarter = block(g, h, dp, ds), block(g, h, dp, ds, piece)
                arrived(whole, ("g", g, h, dp, ds, 0))
                push(quarter, quarter, node(h, 0, onward), ("g", g, h, dp, 2, piece))
                push(whole, whole, (z, sibling), ("s", g, h, dp, ds))

    def gather_four(g, dp):
        for h in range(2):
            for piece in range(2):
                arrived(block(g, h, dp, 2, piece), ("g", g, h, dp, 2, piece))
            whole = block(g, h, dp, 2)
            push(whole, whole, (z, sibling), ("s", g, h, dp, 2))

    def gather_five(g):
        for h in range(2):
            for dp in range(SIDE):
                for ds in range(SIDE):
                    arrived(block(g, h, dp, ds, None, other), ("s", g, h, dp, ds))

    def wide_weights(which, weight, codes_ref, first_group, last_group):
        @pl.loop(first_group, last_group)
        def _(group):
            for hidden_at in range(hidden_count):
                lanes = pl.ds(hidden_at * BLK, BLK)
                codes = codes_ref[pl.ds(pl.multiple_of(group * 8, 8), 8), lanes]
                scales = take_scales(codes, table_ref)
                for inner in range(4):
                    at = group * 4 + inner
                    rows = pl.ds(pl.multiple_of(at * BLK, BLK), BLK)
                    slot = picks[(which * width_count + at) * hidden_count + hidden_at]
                    weight[rows, lanes] = scale_tile(
                        weight[rows, lanes], scales[2 * inner : 2 * inner + 1],
                        scales[2 * inner + 1 : 2 * inner + 2], deltas[slot],
                    )

    def down_weights(first_at, last_at):
        @pl.loop(first_at, last_at)
        def _(at):
            lanes = pl.ds(pl.multiple_of(at * BLK, BLK), BLK)
            scales = take_scales(down_codes[:, lanes], table_ref)
            for hidden_at in range(hidden_count):
                rows = pl.ds(hidden_at * BLK, BLK)
                slot = picks[(2 * width_count + at) * hidden_count + hidden_at]
                down_w[rows, lanes] = scale_tile(
                    down_w[rows, lanes], scales[2 * hidden_at : 2 * hidden_at + 1],
                    scales[2 * hidden_at + 1 : 2 * hidden_at + 2], deltas[slot],
                )

    def across(first, count):
        return jnp.concatenate([held[first + at] for at in range(count)], axis=1)

    def project(weight, into):
        into[...] = jnp.zeros_like(into)

        @pl.loop(0, width_count // 8)
        def _(step):
            rows = pl.ds(pl.multiple_of(step * 8 * BLK, BLK), 8 * BLK)
            into[...] += jnp.dot(
                across(step * 8, 8), weight[rows, :], preferred_element_type=jnp.float32
            )

    def activate():
        @pl.loop(0, tokens // BLK)
        def _(chunk):
            rows = pl.ds(pl.multiple_of(chunk * BLK, BLK), BLK)
            for at in range(hidden_count):
                lanes = pl.ds(at * BLK, BLK)
                gate, up = gate_pre[rows, lanes], up_pre[rows, lanes]
                sig = 1.0 / (1.0 + jnp.exp(-gate))
                gated = gate * sig
                held[2 * tensor + at, rows] = (gated * up).astype(jnp.bfloat16)
                gate_pre[rows, lanes] = gated
                up_pre[rows, lanes] = up * sig * (1.0 + gate * (1.0 - sig))

    def back_hidden():
        grad_hidden[...] = jnp.zeros_like(grad_hidden)

        @pl.loop(0, width_count // 8)
        def _(step):
            lanes = pl.ds(pl.multiple_of(step * 8 * BLK, BLK), 8 * BLK)
            grad_hidden[...] += lax.dot_general(
                across(tensor + step * 8, 8), down_w[:, lanes], contract_last,
                preferred_element_type=jnp.float32,
            )

    def back_gates():
        @pl.loop(0, tokens // BLK)
        def _(chunk):
            rows = pl.ds(pl.multiple_of(chunk * BLK, BLK), BLK)
            for at in range(hidden_count):
                lanes = pl.ds(at * BLK, BLK)
                grad = grad_hidden[rows, lanes]
                held[2 * tensor + hidden_count + at, rows] = (grad * up_pre[rows, lanes]).astype(
                    jnp.bfloat16
                )
                held[2 * tensor + 2 * hidden_count + at, rows] = (
                    grad * gate_pre[rows, lanes]
                ).astype(jnp.bfloat16)

    parts, pairs = (out_parts, input_parts), (out_pair, input_pair)

    def share(r, row, col):
        chip = row * SIDE + col
        if r == 0:
            columns = pl.ds(pl.multiple_of(chip * 2 * BLK, 2 * BLK), 2 * BLK)
            return jnp.dot(
                across(2 * tensor, hidden_count), down_w[:, columns],
                preferred_element_type=jnp.float32,
            )
        rows = pl.ds(pl.multiple_of(chip * 2 * BLK, 2 * BLK), 2 * BLK)
        return lax.dot_general(
            across(2 * tensor + hidden_count, hidden_count), gate_w[rows, :], contract_last,
            preferred_element_type=jnp.float32,
        ) + lax.dot_general(
            across(2 * tensor + 2 * hidden_count, hidden_count), up_w[rows, :], contract_last,
            preferred_element_type=jnp.float32,
        )

    def pair_copy(r, row, col, at):
        return pltpu.make_async_remote_copy(
            src_ref=parts[r].at[row, col, other], dst_ref=pairs[r].at[row, col],
            send_sem=pair_send.at[r * SIDE * SIDE + at], recv_sem=pair_recv.at[r * SIDE * SIDE + at],
            device_id=(z, sibling), device_id_type=MESH,
        )

    def three(at):
        return at + lax.div(at, 2)

    orders = (
        (SIDE, lambda at: (2, at)),
        (SIDE - 1, lambda at: (three(at), 2)),
        ((SIDE - 1) ** 2, lambda at: (three(lax.div(at, SIDE - 1)), three(lax.rem(at, SIDE - 1)))),
    )

    def make_parts(r, order):
        count, steps = orders[order]

        @pl.loop(0, count)
        def _(at):
            dy, dx = steps(at)
            row, col = lax.rem(y + dy, SIDE), lax.rem(x + dx, SIDE)
            both = share(r, row, col).astype(jnp.bfloat16)
            parts[r][row, col, 0] = both[:, :BLK]
            parts[r][row, col, 1] = both[:, BLK:]
            pair_copy(r, row, col, dy * SIDE + dx).start()

    def add_pairs(r, order):
        count, steps = orders[order]

        @pl.loop(0, count)
        def _(at):
            dy, dx = steps(at)
            row, col = lax.rem(y + dy, SIDE), lax.rem(x + dx, SIDE)
            pair_copy(r, row, col, dy * SIDE + dx).wait()
            parts[r][row, col, core] = (
                parts[r][row, col, core].astype(jnp.float32)
                + pairs[r][row, col].astype(jnp.float32)
            ).astype(jnp.bfloat16)

    def cell(r, h, df, dg, piece=None):
        rows = pl.ds(h * half, half) if piece is None else pl.ds(h * half + piece * part, part)
        dy, dx = (df, dg) if h == 0 else (dg, df)
        return parts[r].at[lax.rem(y + dy, SIDE), lax.rem(x + dx, SIDE), core, rows]

    def chip(h, df, dg):
        return (z, spot(df, dg) if h == 0 else spot(dg, df))

    def add_into(target, *terms):
        total = target[...].astype(jnp.float32)
        for term in terms:
            total = total + term[...].astype(jnp.float32)
        target[...] = total.astype(jnp.bfloat16)

    ways = ((0, 1), (1, 3))
    across_order = (2, 1, 3, 0)

    def reduce_one(r, h):
        for dg in across_order:
            for piece, onward in ways:
                push(cell(r, h, 2, dg, piece), far_one.at[r, h, piece, dg], chip(h, onward, 0), ("a", r, h, piece, dg))

    def reduce_two(r, dg):
        for h in range(2):
            for piece, onward in ways:
                landed = far_one.at[r, h, piece, dg]
                arrived(landed, ("a", r, h, piece, dg))
                add_into(cell(r, h, onward, dg, piece), landed)
                push(cell(r, h, onward, dg), far_all.at[r, h, piece, dg], chip(h, onward, 0), ("b", r, h, piece, dg))

    def far_sum(r, h, dg):
        for piece in range(2):
            arrived(far_all.at[r, h, piece, dg], ("b", r, h, piece, dg))
        add_into(cell(r, h, 0, dg), far_all.at[r, h, 0, dg], far_all.at[r, h, 1, dg])

    def reduce_three(r):
        for h in range(2):
            far_sum(r, h, 2)
            for piece, onward in ways:
                push(cell(r, h, 0, 2, piece), near_one.at[r, h, piece], chip(h, 0, onward), ("c", r, h, piece))

    def reduce_four(r):
        for h in range(2):
            for piece, onward in ways:
                far_sum(r, h, onward)
                arrived(near_one.at[r, h, piece], ("c", r, h, piece))
                add_into(cell(r, h, 0, onward, piece), near_one.at[r, h, piece])
                push(cell(r, h, 0, onward), near_all.at[r, h, piece], chip(h, 0, onward), ("d", r, h, piece))

    def reduce_five(r, result):
        for h in range(2):
            far_sum(r, h, 0)
        for h in range(2):
            for piece in range(2):
                arrived(near_all.at[r, h, piece], ("d", r, h, piece))
            result[pl.ds(h * half, half), :] = (
                cell(r, h, 0, 0)[...].astype(jnp.float32)
                + near_all[r, h, 0].astype(jnp.float32)
                + near_all[r, h, 1].astype(jnp.float32)
            ).astype(jnp.bfloat16)

    def block_grads():
        base = 3 * width_count * hidden_count

        @pl.loop(0, groups)
        def _(slot):
            grads[slot] = lax.dot_general(
                held[picks[base + slot]], held[picks[base + groups + slot]], contract_first,
                preferred_element_type=jnp.float32,
            ).astype(jnp.bfloat16)

        for step in range(1, groups):
            to = lax.rem(z + step, groups)
            push(grads.at[to], grads_in.at[step - 1], (to, t), ("h", step))

    def adam():
        total = grads[z].astype(jnp.float32)
        for step in range(1, groups):
            arrived(grads_in.at[step - 1], ("h", step))
            total = total + grads_in[step - 1].astype(jnp.float32)
        moment = beta_one * first_ref[0, 0].astype(jnp.float32) + (1.0 - beta_one) * total
        second = (
            beta_two * second_ref[0, 0].astype(jnp.float32) + (1.0 - beta_two) * total * total
        )
        bias_one = 1.0 - beta_one**ADAM_STEP
        bias_two = 1.0 - beta_two**ADAM_STEP
        step_size = learn_rate * (moment / bias_one) / (jnp.sqrt(second / bias_two) + adam_eps)
        new_delta[0, 0] = delta_ref[0, 0] - step_size
        new_first[0, 0] = moment.astype(jnp.bfloat16)
        new_second[0, 0] = second.astype(jnp.bfloat16)

    gather_zero(0)
    for step in range(1, groups):
        push(deltas.at[z], deltas.at[z], (lax.rem(z + step, groups), t), ("w", step))
    loads[1].wait()
    gather_zero(1)
    gather_one(0)
    gather_three(0, 0)
    for load in loads[2:4]:
        load.wait()
    for step in range(1, groups):
        arrived(deltas.at[lax.rem(z + groups - step, groups)], ("w", step))
    wide_weights(0, gate_w, gate_codes, 0, 2)
    gather_two(0)
    wide_weights(0, gate_w, gate_codes, 2, 5)
    gather_three(0, 3)
    gather_three(0, 1)
    gather_one(1)
    wide_weights(0, gate_w, gate_codes, 5, 8)
    gather_three(0, 2)
    gather_four(0, 0)
    for load in loads[4:6]:
        load.wait()
    wide_weights(1, up_w, up_codes, 0, 4)
    gather_four(0, 3)
    gather_four(0, 1)
    gather_three(1, 0)
    wide_weights(1, up_w, up_codes, 4, 8)
    gather_four(0, 2)
    gather_two(1)
    gather_five(0)
    project(gate_w, gate_pre)
    gather_three(1, 3)
    gather_three(1, 1)
    gather_four(1, 0)
    project(up_w, up_pre)
    gather_three(1, 2)
    gather_four(1, 3)
    gather_four(1, 1)
    activate()
    for load in loads[6:8]:
        load.wait()
    down_weights(0, width_count)
    gather_four(1, 2)
    for order in range(3):
        make_parts(0, order)
    for order in range(2):
        add_pairs(0, order)
    for h in range(2):
        reduce_one(0, h)
    add_pairs(0, 2)
    gather_five(1)
    back_hidden()
    for dg in across_order:
        reduce_two(0, dg)
    back_gates()
    make_parts(1, 0)
    make_parts(1, 1)
    reduce_three(0)
    for order in range(2):
        add_pairs(1, order)
    for h in range(2):
        reduce_one(1, h)
    make_parts(1, 2)
    reduce_four(0)
    add_pairs(1, 2)
    for dg in across_order:
        reduce_two(1, dg)
    block_grads()
    reduce_five(0, out_ref)
    reduce_three(1)
    reduce_four(1)
    adam()
    reduce_five(1, input_ref)
    for copy in sends:
        copy.wait_send()
    assert len(sends) <= SEMAPHORES and len(indices) <= SEMAPHORES


def hand_over(*refs):
    count = len(refs) // 2
    for at in range(count):
        refs[count + at][...] = refs[at][...]


def slot_picks(pattern, width_count, hidden_count, hidden_first):
    slots = pattern.shape[0]
    matrix, width_at, hidden_at = pattern[:, 0], pattern[:, 1], pattern[:, 2] - hidden_first
    place = (matrix * width_count + width_at) * hidden_count + hidden_at
    tiles = jnp.arange(3 * width_count * hidden_count, dtype=jnp.int32)
    found = jnp.where(
        place[:, None] == tiles[None, :], jnp.arange(slots, dtype=jnp.int32)[:, None], slots
    )
    base = 2 * width_count
    left = jnp.where(matrix == 2, base + hidden_at, width_at)
    right = jnp.where(
        matrix == 2, width_count + width_at, base + (1 + matrix) * hidden_count + hidden_at
    )
    return jnp.concatenate([jnp.min(found, axis=0), left, right])


def local(
    groups,
    activations, cotangent, gate_levels, up_levels, down_levels, gate_scales, up_scales, down_scales,
    scale_table, block_pattern, delta_master, first_moment, second_moment,
):
    tokens = activations.shape[0]
    width, hidden = gate_levels.shape
    width_count, hidden_count = width // BLK, hidden // BLK
    half, part = tokens // 2, tokens // 4
    picks = slot_picks(
        block_pattern[0], width_count, hidden_count, lax.axis_index("tensor") * hidden_count
    )
    vmem = pl.BlockSpec(memory_space=pltpu.VMEM)
    anywhere = pl.BlockSpec(memory_space=pl.ANY)
    narrow, wide = jnp.bfloat16, jnp.float32
    shapes = [
        jax.ShapeDtypeStruct(v.shape, v.dtype)
        for v in (activations, activations, delta_master, first_moment, second_moment)
    ]
    results = pl.pallas_call(
        functools.partial(layer_kernel, groups),
        out_shape=shapes,
        in_specs=[anywhere] * 8 + [vmem]
        + [pl.BlockSpec(memory_space=pltpu.SMEM), vmem, vmem, vmem],
        out_specs=[vmem] * 5,
        scratch_shapes=[
            pltpu.VMEM((2 * width_count + 3 * hidden_count, tokens, BLK), narrow),
            pltpu.VMEM((width, hidden), narrow),
            pltpu.VMEM((width, hidden), narrow),
            pltpu.VMEM((hidden, width), narrow),
            pltpu.VMEM(gate_scales.shape, jnp.int32),
            pltpu.VMEM(up_scales.shape, jnp.int32),
            pltpu.VMEM(down_scales.shape, jnp.int32),
            pltpu.VMEM((tokens, hidden), wide),
            pltpu.VMEM((tokens, hidden), wide),
            pltpu.VMEM((tokens, hidden), wide),
            pltpu.VMEM((groups + 1, BLK, BLK), narrow),
            pltpu.VMEM((SIDE, SIDE, CORES, tokens, BLK), narrow),
            pltpu.VMEM((SIDE, SIDE, CORES, tokens, BLK), narrow),
            pltpu.VMEM((SIDE, SIDE, tokens, BLK), narrow),
            pltpu.VMEM((SIDE, SIDE, tokens, BLK), narrow),
            pltpu.VMEM((2, 2, 2, SIDE, part, BLK), narrow),
            pltpu.VMEM((2, 2, 2, SIDE, half, BLK), narrow),
            pltpu.VMEM((2, 2, 2, part, BLK), narrow),
            pltpu.VMEM((2, 2, 2, half, BLK), narrow),
            pltpu.VMEM((groups, BLK, BLK), narrow),
            pltpu.VMEM((groups - 1, BLK, BLK), narrow),
            pltpu.SemaphoreType.DMA((SEMAPHORES,)),
            pltpu.SemaphoreType.DMA((SEMAPHORES,)),
            pltpu.SemaphoreType.DMA((2 * SIDE * SIDE,)),
            pltpu.SemaphoreType.DMA((2 * SIDE * SIDE,)),
            pltpu.SemaphoreType.DMA((8,)),
        ],
        compiler_params=pltpu.CompilerParams(
            collective_id=0, has_side_effects=True, vmem_limit_bytes=58 * 1024 * 1024
        ),
        cost_estimate=pl.CostEstimate(
            flops=13_000_000_000, bytes_accessed=14_000_000, transcendentals=262_144
        ),
    )(
        activations, cotangent, gate_levels, up_levels, down_levels, gate_scales, up_scales,
        down_scales, scale_table.reshape(1, 256), picks, delta_master, first_moment, second_moment,
    )
    return pl.pallas_call(
        hand_over,
        out_shape=shapes,
        in_specs=[vmem] * 5,
        out_specs=[vmem] * 5,
    )(*results)


def solution(mesh):
    in_specs = (
        P("dp", "tensor"),
        P("dp", "tensor"),
        P(None, "tensor"),
        P(None, "tensor"),
        P("tensor", None),
        P(None, "tensor"),
        P(None, "tensor"),
        P("tensor", None),
        P(),
        P("tensor", None, None),
        P("tensor", "dp", None, None),
        P("tensor", "dp", None, None),
        P("tensor", "dp", None, None),
    )
    out_specs = (
        P("dp", "tensor"),
        P("dp", "tensor"),
        P("tensor", "dp", None, None),
        P("tensor", "dp", None, None),
        P("tensor", "dp", None, None),
    )
    return jax.shard_map(
        functools.partial(local, mesh.shape["dp"]),
        mesh=mesh, in_specs=in_specs, out_specs=out_specs, check_vma=False,
    )
```

```python
import functools

import jax
import jax.numpy as jnp
from jax import lax
from jax.experimental import pallas as pl
from jax.experimental.pallas import tpu as pltpu
from jax.sharding import PartitionSpec as P

BLK = 128
QBLK = 64
ADAM_STEP = 20
SIDE = 4
CORES = 2
SENDS = 14
ARRIVALS = 54

beta_one = 0.9
beta_two = 0.999
adam_eps = 1e-08
learn_rate = 0.05

MESH = pl.DeviceIdType.MESH
contract_last = (((1,), (1,)), ((), ()))
contract_first = (((0,), (0,)), ((), ()))


def take_scales(codes, table_ref):
    low = jnp.broadcast_to(table_ref[0:1, 0:128], codes.shape)
    high = jnp.broadcast_to(table_ref[0:1, 128:256], codes.shape)
    within = jnp.bitwise_and(codes, 127)
    from_low = jnp.take_along_axis(low, within, axis=1, mode="promise_in_bounds")
    from_high = jnp.take_along_axis(high, within, axis=1, mode="promise_in_bounds")
    return jnp.where(codes < 128, from_low, from_high)


def scale_tile(levels, upper, lower):
    scales = jnp.concatenate(
        [jnp.broadcast_to(upper, (QBLK, BLK)), jnp.broadcast_to(lower, (QBLK, BLK))], axis=0
    )
    return (levels.astype(jnp.float32) * scales).astype(jnp.bfloat16)


def add_block(base, block):
    return (base.astype(jnp.float32) + block.astype(jnp.float32)).astype(jnp.bfloat16)


def layer_kernel(
    groups,
    x_ref, dy_ref, gate_levels, up_levels, down_levels, gate_scales, up_scales, down_scales, table_ref,
    picks, delta_ref, first_ref, second_ref,
    out_ref, input_ref, new_delta, new_first, new_second,
    first, second, held, gate_w, up_w, down_w, gate_codes, up_codes, down_codes, gate_pre, up_pre, grad_hidden, deltas,
    out_parts, input_parts, out_pair, input_pair, far_one, far_all, near_one, near_all,
    grads, grads_in, send_sem, recv_sem, load_sem,
):
    tokens = x_ref.shape[0]
    hidden_count = gate_w.shape[1] // BLK
    width_count = gate_w.shape[0] // BLK
    tensor = width_count
    half, part = tokens // 2, tokens // 4
    z, t = lax.axis_index("dp"), lax.axis_index("tensor")
    core = lax.rem(t, CORES)
    x = lax.rem(lax.div(t, CORES), SIDE)
    y = lax.div(t, CORES * SIDE)

    def spot(dy, dx, which=None):
        row, col = lax.rem(y + dy, SIDE), lax.rem(x + dx, SIDE)
        return (row * SIDE + col) * CORES + (core if which is None else which)

    other = 1 - core
    sibling = spot(0, 0, other)

    leaving, landing = {}, {}

    def copy_of(src, dst, to, send_key, recv_key):
        return pltpu.make_async_remote_copy(
            src_ref=src, dst_ref=dst, send_sem=send_sem.at[leaving.setdefault(send_key, len(leaving))],
            recv_sem=recv_sem.at[landing.setdefault(recv_key, len(landing))],
            device_id=to, device_id_type=MESH,
        )

    def push(src, dst, to, send_key, recv_key):
        copy_of(src, dst, to, send_key, recv_key).start()

    def arrived(like, recv_key):
        pltpu.make_async_remote_copy(
            src_ref=like, dst_ref=like, send_sem=send_sem.at[0],
            recv_sem=recv_sem.at[landing.setdefault(recv_key, len(landing))],
            device_id=(z, sibling), device_id_type=MESH,
        ).wait_recv()

    def left(like, send_key):
        pltpu.make_async_remote_copy(
            src_ref=like, dst_ref=like, send_sem=send_sem.at[leaving[send_key]],
            recv_sem=recv_sem.at[0], device_id=(z, sibling), device_id_type=MESH,
        ).wait_send()

    loads = [
        pltpu.make_async_copy(src, dst, load_sem.at[at])
        for at, (src, dst) in enumerate(
            (
                (x_ref, held.at[t]), (dy_ref, held.at[tensor + t]),
                (down_scales, down_codes), (down_levels, down_w),
                (gate_scales, gate_codes), (gate_levels, gate_w),
                (up_scales, up_codes), (up_levels, up_w),
                (first_ref, first), (second_ref, second),
            )
        )
    ]
    for load in loads:
        load.start()
    barrier = pltpu.get_barrier_semaphore()
    partners = [(z, spot(0, 1)), (z, spot(0, 3)), (z, spot(1, 0)), (z, spot(3, 0)), (z, sibling)]
    partners += [(lax.rem(z + step, groups), t) for step in range(1, groups)]
    for partner in partners:
        pl.semaphore_signal(barrier, inc=1, device_id=partner, device_id_type=MESH)
    deltas[z] = delta_ref[0, 0].astype(jnp.bfloat16)
    deltas[groups] = jnp.zeros((BLK, BLK), jnp.bfloat16)
    loads[0].wait()
    pl.semaphore_wait(barrier, len(partners))

    def block(g, h, dp, ds, piece=None, which=None):
        at = spot(ds, dp, which) if h == 0 else spot(dp, ds, which)
        rows = pl.ds(h * half, half) if piece is None else pl.ds(h * half + piece * part, part)
        return held.at[g * tensor + at, rows]

    def node(h, dp, ds):
        return (z, spot(ds, dp) if h == 0 else spot(dp, ds))

    def spread(g, h, dp):
        whole = block(g, h, dp, 0)
        push(whole, whole, node(h, 0, 1), ("g", g), ("three", g, dp))
        push(whole, whole, node(h, 0, 3), ("g", g), ("three", g, dp))
        push(whole, whole, (z, sibling), ("g", g), ("five", g))

    def blocks_of(g, count):
        return held.at[pl.ds(g * tensor, count)]

    def gather_zero(g):
        for h in range(2):
            whole = block(g, h, 0, 0)
            push(whole, whole, node(h, 1, 0), ("g", g), ("one", g))
            push(whole, whole, node(h, 3, 0), ("g", g), ("one", g))
        for h in range(2):
            spread(g, h, 0)

    def gather_one(g):
        arrived(blocks_of(g, 2), ("one", g))
        for h in range(2):
            for dp, piece, onward in ((3, 0, 1), (1, 1, 3)):
                quarter = block(g, h, dp, 0, piece)
                push(quarter, quarter, node(h, onward, 0), ("g", g), ("two", g))
        for h in range(2):
            for dp in (3, 1):
                spread(g, h, dp)

    def gather_two(g):
        arrived(blocks_of(g, 1), ("two", g))
        for h in range(2):
            spread(g, h, 2)

    def gather_three(g, dp):
        arrived(blocks_of(g, 2), ("three", g, dp))
        for h in range(2):
            for ds, piece, onward in ((3, 0, 1), (1, 1, 3)):
                quarter = block(g, h, dp, ds, piece)
                push(quarter, quarter, node(h, 0, onward), ("g", g), ("four", g, dp))
        for h in range(2):
            for ds in (3, 1):
                whole = block(g, h, dp, ds)
                push(whole, whole, (z, sibling), ("g", g), ("five", g))

    def gather_four(g, dp):
        arrived(blocks_of(g, 1), ("four", g, dp))
        for h in range(2):
            whole = block(g, h, dp, 2)
            push(whole, whole, (z, sibling), ("g", g), ("five", g))

    def gather_five(g):
        arrived(blocks_of(g, tensor // 2), ("five", g))

    def wide_weights(which, weight, codes_ref, first_group, last_group):
        @pl.loop(first_group, last_group)
        def _(group):
            for hidden_at in range(hidden_count):
                lanes = pl.ds(hidden_at * BLK, BLK)
                codes = codes_ref[pl.ds(pl.multiple_of(group * 8, 8), 8), lanes]
                scales = take_scales(codes, table_ref)
                for inner in range(4):
                    at = group * 4 + inner
                    rows = pl.ds(pl.multiple_of(at * BLK, BLK), BLK)
                    slot = picks[(which * width_count + at) * hidden_count + hidden_at]
                    base = scale_tile(
                        weight[rows, lanes], scales[2 * inner : 2 * inner + 1],
                        scales[2 * inner + 1 : 2 * inner + 2],
                    )
                    weight[rows, lanes] = add_block(base, deltas[slot])

    def down_base(first_group, last_group):
        @pl.loop(first_group, last_group)
        def _(group):
            for inner in range(4):
                lanes = pl.ds(pl.multiple_of((group * 4 + inner) * BLK, BLK), BLK)
                scales = take_scales(down_codes[:, lanes], table_ref)
                for hidden_at in range(hidden_count):
                    rows = pl.ds(hidden_at * BLK, BLK)
                    down_w[rows, lanes] = scale_tile(
                        down_w[rows, lanes], scales[2 * hidden_at : 2 * hidden_at + 1],
                        scales[2 * hidden_at + 1 : 2 * hidden_at + 2],
                    )

    def down_blocks(first_group, last_group):
        @pl.loop(first_group, last_group)
        def _(group):
            for inner in range(4):
                at = group * 4 + inner
                lanes = pl.ds(pl.multiple_of(at * BLK, BLK), BLK)
                for hidden_at in range(hidden_count):
                    rows = pl.ds(hidden_at * BLK, BLK)
                    slot = picks[(2 * width_count + at) * hidden_count + hidden_at]
                    down_w[rows, lanes] = add_block(down_w[rows, lanes], deltas[slot])

    def across(first, count):
        return jnp.concatenate([held[first + at] for at in range(count)], axis=1)

    def project(weight, into, first_step, last_step):
        if first_step == 0:
            into[...] = jnp.zeros_like(into)

        @pl.loop(first_step, last_step)
        def _(step):
            rows = pl.ds(pl.multiple_of(step * 8 * BLK, BLK), 8 * BLK)
            into[...] += jnp.dot(
                across(step * 8, 8), weight[rows, :], preferred_element_type=jnp.float32
            )

    def activate():
        @pl.loop(0, tokens // BLK)
        def _(chunk):
            rows = pl.ds(pl.multiple_of(chunk * BLK, BLK), BLK)
            for at in range(hidden_count):
                lanes = pl.ds(at * BLK, BLK)
                gate, up = gate_pre[rows, lanes], up_pre[rows, lanes]
                sig = 1.0 / (1.0 + jnp.exp(-gate))
                gated = gate * sig
                held[2 * tensor + at, rows] = (gated * up).astype(jnp.bfloat16)
                gate_pre[rows, lanes] = gated
                up_pre[rows, lanes] = up * sig * (1.0 + gate * (1.0 - sig))

    def back_hidden():
        grad_hidden[...] = jnp.zeros_like(grad_hidden)

        @pl.loop(0, width_count // 8)
        def _(step):
            lanes = pl.ds(pl.multiple_of(step * 8 * BLK, BLK), 8 * BLK)
            grad_hidden[...] += lax.dot_general(
                across(tensor + step * 8, 8), down_w[:, lanes], contract_last,
                preferred_element_type=jnp.float32,
            )

    def back_gates():
        @pl.loop(0, tokens // BLK)
        def _(chunk):
            rows = pl.ds(pl.multiple_of(chunk * BLK, BLK), BLK)
            for at in range(hidden_count):
                lanes = pl.ds(at * BLK, BLK)
                grad = grad_hidden[rows, lanes]
                held[2 * tensor + hidden_count + at, rows] = (grad * up_pre[rows, lanes]).astype(
                    jnp.bfloat16
                )
                held[2 * tensor + 2 * hidden_count + at, rows] = (
                    grad * gate_pre[rows, lanes]
                ).astype(jnp.bfloat16)

    parts, pairs = (out_parts, input_parts), (out_pair, input_pair)

    def share(r, row, col):
        chip = row * SIDE + col
        if r == 0:
            columns = pl.ds(pl.multiple_of(chip * 2 * BLK, 2 * BLK), 2 * BLK)
            return jnp.dot(
                across(2 * tensor, hidden_count), down_w[:, columns],
                preferred_element_type=jnp.float32,
            )
        rows = pl.ds(pl.multiple_of(chip * 2 * BLK, 2 * BLK), 2 * BLK)
        return lax.dot_general(
            across(2 * tensor + hidden_count, 2 * hidden_count),
            jnp.concatenate([gate_w[rows, :], up_w[rows, :]], axis=1), contract_last,
            preferred_element_type=jnp.float32,
        )

    def odd(at):
        return 1 + 2 * lax.rem(at, 2)

    orders = (
        (4, lambda at: (2, at)),
        (3, lambda at: (at + lax.div(at, 2), 2)),
        (4, lambda at: (1 + 2 * lax.div(at, 2), odd(at))),
        (4, lambda at: (odd(at) * (1 - lax.div(at, 2)), odd(at) * lax.div(at, 2))),
        (1, lambda at: (at, at)),
    )

    def make_parts(r, order):
        count, steps = orders[order]
        each = 2 if count % 2 == 0 else count

        def some(first):
            spots = []
            for at in range(each):
                dy, dx = steps(first + at)
                spots.append((lax.rem(y + dy, SIDE), lax.rem(x + dx, SIDE)))
            for row, col in spots:
                both = share(r, row, col).astype(jnp.bfloat16)
                parts[r][row, col, 0] = both[:, :BLK]
                parts[r][row, col, 1] = both[:, BLK:]
            for row, col in spots:
                push(parts[r].at[row, col, other], pairs[r].at[row, col], (z, sibling), ("p", r), ("p", r, order))

        if each == count:
            some(jnp.int32(0))
        else:
            pl.loop(0, count // each)(lambda at: some(at * each))

    def add_pairs(r, order):
        count, steps = orders[order]
        arrived(pairs[r].at[0, pl.ds(0, count)], ("p", r, order))

        @pl.loop(0, count)
        def _(at):
            dy, dx = steps(at)
            row, col = lax.rem(y + dy, SIDE), lax.rem(x + dx, SIDE)
            parts[r][row, col, core] = (
                parts[r][row, col, core].astype(jnp.float32)
                + pairs[r][row, col].astype(jnp.float32)
            ).astype(jnp.bfloat16)

    def cell(r, h, df, dg, piece=None):
        rows = pl.ds(h * half, half) if piece is None else pl.ds(h * half + piece * part, part)
        dy, dx = (df, dg) if h == 0 else (dg, df)
        return parts[r].at[lax.rem(y + dy, SIDE), lax.rem(x + dx, SIDE), core, rows]

    def chip(h, df, dg):
        return (z, spot(df, dg) if h == 0 else spot(dg, df))

    def add_into(target, *terms):
        total = target[...].astype(jnp.float32)
        for term in terms:
            total = total + term[...].astype(jnp.float32)
        target[...] = total.astype(jnp.bfloat16)

    ways = ((0, 1), (1, 3))
    across_order = (2, 1, 3, 0)

    def reduce_one(r):
        for dg in across_order:
            for h in range(2):
                for piece, onward in ways:
                    push(cell(r, h, 2, dg, piece), far_one.at[r, dg, h, piece], chip(h, onward, 0), ("a", r), ("a", r, dg))

    def reduce_two(r, dg):
        arrived(far_one.at[r, dg], ("a", r, dg))
        for h in range(2):
            for piece, onward in ways:
                add_into(cell(r, h, onward, dg, piece), far_one.at[r, dg, h, piece])
                push(cell(r, h, onward, dg), far_all.at[r, dg, h, piece], chip(h, onward, 0), ("b", r), ("b", r, dg))

    def far_sum(r, dg):
        arrived(far_all.at[r, dg], ("b", r, dg))
        for h in range(2):
            add_into(cell(r, h, 0, dg), far_all.at[r, dg, h, 0], far_all.at[r, dg, h, 1])

    def reduce_three(r):
        far_sum(r, 2)
        for h in range(2):
            for piece, onward in ways:
                push(cell(r, h, 0, 2, piece), near_one.at[r, h, piece], chip(h, 0, onward), ("c", r), ("c", r))

    def reduce_four(r):
        far_sum(r, 1)
        far_sum(r, 3)
        arrived(near_one.at[r], ("c", r))
        for h in range(2):
            for piece, onward in ways:
                add_into(cell(r, h, 0, onward, piece), near_one.at[r, h, piece])
                push(cell(r, h, 0, onward), near_all.at[r, h, piece], chip(h, 0, onward), ("d", r), ("d", r))

    def reduce_five(r, result):
        far_sum(r, 0)
        arrived(near_all.at[r], ("d", r))
        for h in range(2):
            result[pl.ds(h * half, half), :] = (
                cell(r, h, 0, 0)[...].astype(jnp.float32)
                + near_all[r, h, 0].astype(jnp.float32)
                + near_all[r, h, 1].astype(jnp.float32)
            ).astype(jnp.bfloat16)

    def block_grads():
        base = 3 * width_count * hidden_count

        @pl.loop(0, groups)
        def _(slot):
            grads[slot] = lax.dot_general(
                held[picks[base + slot]], held[picks[base + groups + slot]], contract_first,
                preferred_element_type=jnp.float32,
            ).astype(jnp.bfloat16)

        for step in range(1, groups):
            to = lax.rem(z + step, groups)
            push(grads.at[to], grads_in.at[step - 1], (to, t), ("h",), ("h",))

    def adam():
        total = grads[z].astype(jnp.float32)
        arrived(grads_in, ("h",))
        for step in range(1, groups):
            total = total + grads_in[step - 1].astype(jnp.float32)
        moment = beta_one * first[0, 0].astype(jnp.float32) + (1.0 - beta_one) * total
        square = (
            beta_two * second[0, 0].astype(jnp.float32) + (1.0 - beta_two) * total * total
        )
        bias_one = 1.0 - beta_one**ADAM_STEP
        bias_two = 1.0 - beta_two**ADAM_STEP
        step_size = learn_rate * (moment / bias_one) / (jnp.sqrt(square / bias_two) + adam_eps)
        new_delta[0, 0] = delta_ref[0, 0] - step_size
        new_first[0, 0] = moment.astype(jnp.bfloat16)
        new_second[0, 0] = square.astype(jnp.bfloat16)

    gather_zero(0)
    for step in range(1, groups):
        push(deltas.at[z], deltas.at[z], (lax.rem(z + step, groups), t), ("w",), ("w",))
    for load in loads[1:4]:
        load.wait()
    down_base(0, 4)
    gather_zero(1)
    down_base(4, 8)
    gather_one(0)
    gather_three(0, 0)
    for load in loads[4:]:
        load.wait()
    gather_two(0)
    arrived(deltas.at[pl.ds(0, groups - 1)], ("w",))
    wide_weights(0, gate_w, gate_codes, 0, 4)
    gather_three(0, 3)
    wide_weights(0, gate_w, gate_codes, 4, 8)
    gather_three(0, 1)
    gather_one(1)
    wide_weights(1, up_w, up_codes, 0, 4)
    gather_four(0, 0)
    gather_three(0, 2)
    wide_weights(1, up_w, up_codes, 4, 8)
    gather_three(1, 0)
    gather_four(0, 3)
    gather_four(0, 1)
    down_blocks(0, 8)
    gather_four(0, 2)
    gather_two(1)
    gather_five(0)
    project(gate_w, gate_pre, 0, 2)
    gather_three(1, 3)
    gather_three(1, 1)
    project(gate_w, gate_pre, 2, 4)
    gather_four(1, 0)
    project(up_w, up_pre, 0, 2)
    gather_three(1, 2)
    project(up_w, up_pre, 2, 4)
    gather_four(1, 3)
    gather_four(1, 1)
    activate()
    make_parts(0, 0)
    gather_four(1, 2)
    make_parts(0, 1)
    add_pairs(0, 0)
    add_pairs(0, 1)
    reduce_one(0)
    gather_five(1)
    back_hidden()
    back_gates()
    make_parts(0, 2)
    add_pairs(0, 2)
    for dg in (2, 1, 3):
        reduce_two(0, dg)
    make_parts(0, 3)
    make_parts(0, 4)
    add_pairs(0, 3)
    add_pairs(0, 4)
    reduce_two(0, 0)
    make_parts(1, 0)
    make_parts(1, 1)
    reduce_three(0)
    add_pairs(1, 0)
    add_pairs(1, 1)
    reduce_one(1)
    make_parts(1, 2)
    reduce_four(0)
    block_grads()
    add_pairs(1, 2)
    for dg in (2, 1, 3):
        reduce_two(1, dg)
    make_parts(1, 3)
    make_parts(1, 4)
    reduce_five(0, out_ref)
    add_pairs(1, 3)
    add_pairs(1, 4)
    reduce_two(1, 0)
    reduce_three(1)
    reduce_four(1)
    adam()
    reduce_five(1, input_ref)
    left(deltas.at[pl.ds(0, groups - 1)], ("w",))
    left(grads_in, ("h",))
    for r in range(2):
        left(blocks_of(r, tensor - 1), ("g", r))
        left(pairs[r], ("p", r))
        left(far_one.at[r], ("a", r))
        left(far_all.at[r], ("b", r))
        left(near_one.at[r], ("c", r))
        left(near_all.at[r], ("d", r))
    assert len(leaving) <= SENDS and len(landing) <= ARRIVALS, (len(leaving), len(landing))


def hand_over(*refs):
    count = len(refs) // 2
    for at in range(count):
        refs[count + at][...] = refs[at][...]


def slot_picks(pattern, width_count, hidden_count, hidden_first):
    slots = pattern.shape[0]
    matrix, width_at, hidden_at = pattern[:, 0], pattern[:, 1], pattern[:, 2] - hidden_first
    place = (matrix * width_count + width_at) * hidden_count + hidden_at
    tiles = jnp.arange(3 * width_count * hidden_count, dtype=jnp.int32)
    found = jnp.where(
        place[:, None] == tiles[None, :], jnp.arange(slots, dtype=jnp.int32)[:, None], slots
    )
    base = 2 * width_count
    left = jnp.where(matrix == 2, base + hidden_at, width_at)
    right = jnp.where(
        matrix == 2, width_count + width_at, base + (1 + matrix) * hidden_count + hidden_at
    )
    return jnp.concatenate([jnp.min(found, axis=0), left, right])


def local(
    groups,
    activations, cotangent, gate_levels, up_levels, down_levels, gate_scales, up_scales, down_scales,
    scale_table, block_pattern, delta_master, first_moment, second_moment,
):
    tokens = activations.shape[0]
    width, hidden = gate_levels.shape
    width_count, hidden_count = width // BLK, hidden // BLK
    half, part = tokens // 2, tokens // 4
    picks = slot_picks(
        block_pattern[0], width_count, hidden_count, lax.axis_index("tensor") * hidden_count
    )
    vmem = pl.BlockSpec(memory_space=pltpu.VMEM)
    anywhere = pl.BlockSpec(memory_space=pl.ANY)
    narrow, wide = jnp.bfloat16, jnp.float32
    shapes = [
        jax.ShapeDtypeStruct(v.shape, v.dtype)
        for v in (activations, activations, delta_master, first_moment, second_moment)
    ]
    results = pl.pallas_call(
        functools.partial(layer_kernel, groups),
        out_shape=shapes,
        in_specs=[anywhere] * 8 + [vmem]
        + [pl.BlockSpec(memory_space=pltpu.SMEM), vmem, anywhere, anywhere],
        out_specs=[vmem] * 5,
        scratch_shapes=[
            pltpu.VMEM(first_moment.shape, narrow),
            pltpu.VMEM(second_moment.shape, narrow),
            pltpu.VMEM((2 * width_count + 3 * hidden_count, tokens, BLK), narrow),
            pltpu.VMEM((width, hidden), narrow),
            pltpu.VMEM((width, hidden), narrow),
            pltpu.VMEM((hidden, width), narrow),
            pltpu.VMEM(gate_scales.shape, jnp.int32),
            pltpu.VMEM(up_scales.shape, jnp.int32),
            pltpu.VMEM(down_scales.shape, jnp.int32),
            pltpu.VMEM((tokens, hidden), wide),
            pltpu.VMEM((tokens, hidden), wide),
            pltpu.VMEM((tokens, hidden), wide),
            pltpu.VMEM((groups + 1, BLK, BLK), narrow),
            pltpu.VMEM((SIDE, SIDE, CORES, tokens, BLK), narrow),
            pltpu.VMEM((SIDE, SIDE, CORES, tokens, BLK), narrow),
            pltpu.VMEM((SIDE, SIDE, tokens, BLK), narrow),
            pltpu.VMEM((SIDE, SIDE, tokens, BLK), narrow),
            pltpu.VMEM((2, SIDE, 2, 2, part, BLK), narrow),
            pltpu.VMEM((2, SIDE, 2, 2, half, BLK), narrow),
            pltpu.VMEM((2, 2, 2, part, BLK), narrow),
            pltpu.VMEM((2, 2, 2, half, BLK), narrow),
            pltpu.VMEM((groups, BLK, BLK), narrow),
            pltpu.VMEM((groups - 1, BLK, BLK), narrow),
            pltpu.SemaphoreType.DMA((SENDS,)),
            pltpu.SemaphoreType.DMA((ARRIVALS,)),
            pltpu.SemaphoreType.DMA((10,)),
        ],
        compiler_params=pltpu.CompilerParams(
            collective_id=0, has_side_effects=True, vmem_limit_bytes=58 * 1024 * 1024
        ),
        cost_estimate=pl.CostEstimate(
            flops=13_000_000_000, bytes_accessed=14_000_000, transcendentals=262_144
        ),
    )(
        activations, cotangent, gate_levels, up_levels, down_levels, gate_scales, up_scales,
        down_scales, scale_table.reshape(1, 256), picks, delta_master, first_moment, second_moment,
    )
    return pl.pallas_call(
        hand_over,
        out_shape=shapes,
        in_specs=[vmem] * 5,
        out_specs=[vmem] * 5,
    )(*results)


def solution(mesh):
    in_specs = (
        P("dp", "tensor"),
        P("dp", "tensor"),
        P(None, "tensor"),
        P(None, "tensor"),
        P("tensor", None),
        P(None, "tensor"),
        P(None, "tensor"),
        P("tensor", None),
        P(),
        P("tensor", None, None),
        P("tensor", "dp", None, None),
        P("tensor", "dp", None, None),
        P("tensor", "dp", None, None),
    )
    out_specs = (
        P("dp", "tensor"),
        P("dp", "tensor"),
        P("tensor", "dp", None, None),
        P("tensor", "dp", None, None),
        P("tensor", "dp", None, None),
    )
    return jax.shard_map(
        functools.partial(local, mesh.shape["dp"]),
        mesh=mesh, in_specs=in_specs, out_specs=out_specs, check_vma=False,
    )
```

```python
import functools

import jax
import jax.numpy as jnp
from jax import lax
from jax.experimental import pallas as pl
from jax.experimental.pallas import tpu as pltpu
from jax.sharding import PartitionSpec as P

BLK = 128
QBLK = 64
ADAM_STEP = 20
SIDE = 4
CORES = 2
SENDS = 14
ARRIVALS = 54

beta_one = 0.9
beta_two = 0.999
adam_eps = 1e-08
learn_rate = 0.05

MESH = pl.DeviceIdType.MESH
contract_last = (((1,), (1,)), ((), ()))
contract_first = (((0,), (0,)), ((), ()))


def take_scales(codes, table_ref):
    low = jnp.broadcast_to(table_ref[0:1, 0:128], codes.shape)
    high = jnp.broadcast_to(table_ref[0:1, 128:256], codes.shape)
    within = jnp.bitwise_and(codes, 127)
    from_low = jnp.take_along_axis(low, within, axis=1, mode="promise_in_bounds")
    from_high = jnp.take_along_axis(high, within, axis=1, mode="promise_in_bounds")
    return jnp.where(codes < 128, from_low, from_high)


def scale_tile(levels, upper, lower):
    scales = jnp.concatenate(
        [jnp.broadcast_to(upper, (QBLK, BLK)), jnp.broadcast_to(lower, (QBLK, BLK))], axis=0
    )
    return (levels.astype(jnp.float32) * scales).astype(jnp.bfloat16)


def add_block(base, block):
    return (base.astype(jnp.float32) + block.astype(jnp.float32)).astype(jnp.bfloat16)


def layer_kernel(
    groups,
    x_ref, dy_ref, gate_levels, up_levels, down_levels, gate_scales, up_scales, down_scales, table_ref,
    picks, delta_ref, first_ref, second_ref,
    out_ref, input_ref, new_delta, new_first, new_second,
    first, second, held, gate_w, up_w, down_w, gate_codes, up_codes, down_codes, gate_pre, up_pre, grad_hidden, deltas,
    out_parts, input_parts, out_pair, input_pair, far_one, far_all, near_one, near_all,
    grads, grads_in, send_sem, recv_sem, load_sem,
):
    tokens = x_ref.shape[0]
    hidden_count = gate_w.shape[1] // BLK
    width_count = gate_w.shape[0] // BLK
    tensor = width_count
    half, part = tokens // 2, tokens // 4
    z, t = lax.axis_index("dp"), lax.axis_index("tensor")
    core = lax.rem(t, CORES)
    x = lax.rem(lax.div(t, CORES), SIDE)
    y = lax.div(t, CORES * SIDE)

    def spot(dy, dx, which=None):
        row, col = lax.rem(y + dy, SIDE), lax.rem(x + dx, SIDE)
        return (row * SIDE + col) * CORES + (core if which is None else which)

    other = 1 - core
    sibling = spot(0, 0, other)

    leaving, landing = {}, {}

    def copy_of(src, dst, to, send_key, recv_key):
        return pltpu.make_async_remote_copy(
            src_ref=src, dst_ref=dst, send_sem=send_sem.at[leaving.setdefault(send_key, len(leaving))],
            recv_sem=recv_sem.at[landing.setdefault(recv_key, len(landing))],
            device_id=to, device_id_type=MESH,
        )

    def push(src, dst, to, send_key, recv_key):
        copy_of(src, dst, to, send_key, recv_key).start()

    def arrived(like, recv_key):
        pltpu.make_async_remote_copy(
            src_ref=like, dst_ref=like, send_sem=send_sem.at[0],
            recv_sem=recv_sem.at[landing.setdefault(recv_key, len(landing))],
            device_id=(z, sibling), device_id_type=MESH,
        ).wait_recv()

    def left(like, send_key):
        pltpu.make_async_remote_copy(
            src_ref=like, dst_ref=like, send_sem=send_sem.at[leaving[send_key]],
            recv_sem=recv_sem.at[0], device_id=(z, sibling), device_id_type=MESH,
        ).wait_send()

    loads = [
        pltpu.make_async_copy(src, dst, load_sem.at[at])
        for at, (src, dst) in enumerate(
            (
                (x_ref, held.at[t]), (dy_ref, held.at[tensor + t]),
                (down_scales, down_codes), (down_levels, down_w),
                (gate_scales, gate_codes), (gate_levels, gate_w),
                (up_scales, up_codes), (up_levels, up_w),
                (first_ref, first), (second_ref, second),
            )
        )
    ]
    for load in loads:
        load.start()
    barrier = pltpu.get_barrier_semaphore()
    partners = [(z, spot(0, 1)), (z, spot(0, 3)), (z, spot(1, 0)), (z, spot(3, 0)), (z, sibling)]
    partners += [(lax.rem(z + step, groups), t) for step in range(1, groups)]
    for partner in partners:
        pl.semaphore_signal(barrier, inc=1, device_id=partner, device_id_type=MESH)
    deltas[z] = delta_ref[0, 0].astype(jnp.bfloat16)
    deltas[groups] = jnp.zeros((BLK, BLK), jnp.bfloat16)
    loads[0].wait()
    pl.semaphore_wait(barrier, len(partners))

    def block(g, h, dp, ds, piece=None, which=None):
        at = spot(ds, dp, which) if h == 0 else spot(dp, ds, which)
        rows = pl.ds(h * half, half) if piece is None else pl.ds(h * half + piece * part, part)
        return held.at[g * tensor + at, rows]

    def node(h, dp, ds):
        return (z, spot(ds, dp) if h == 0 else spot(dp, ds))

    def spread(g, h, dp):
        whole = block(g, h, dp, 0)
        push(whole, whole, node(h, 0, 1), ("g", g), ("three", g, dp))
        push(whole, whole, node(h, 0, 3), ("g", g), ("three", g, dp))
        push(whole, whole, (z, sibling), ("g", g), ("five", g))

    def blocks_of(g, count):
        return held.at[pl.ds(g * tensor, count)]

    def gather_zero(g):
        for h in range(2):
            whole = block(g, h, 0, 0)
            push(whole, whole, node(h, 1, 0), ("g", g), ("one", g))
            push(whole, whole, node(h, 3, 0), ("g", g), ("one", g))

    def spread_own(g):
        for h in range(2):
            spread(g, h, 0)

    def gather_one(g):
        arrived(blocks_of(g, 2), ("one", g))
        for h in range(2):
            for dp, piece, onward in ((3, 0, 1), (1, 1, 3)):
                quarter = block(g, h, dp, 0, piece)
                push(quarter, quarter, node(h, onward, 0), ("g", g), ("two", g))
        for h in range(2):
            for dp in (3, 1):
                spread(g, h, dp)

    def gather_two(g):
        arrived(blocks_of(g, 1), ("two", g))
        for h in range(2):
            spread(g, h, 2)

    def gather_three(g, dp):
        arrived(blocks_of(g, 2), ("three", g, dp))
        for h in range(2):
            for ds, piece, onward in ((3, 0, 1), (1, 1, 3)):
                quarter = block(g, h, dp, ds, piece)
                push(quarter, quarter, node(h, 0, onward), ("g", g), ("four", g, dp))
        for h in range(2):
            for ds in (3, 1):
                whole = block(g, h, dp, ds)
                push(whole, whole, (z, sibling), ("g", g), ("five", g))

    def gather_four(g, dp):
        arrived(blocks_of(g, 1), ("four", g, dp))
        for h in range(2):
            whole = block(g, h, dp, 2)
            push(whole, whole, (z, sibling), ("g", g), ("five", g))

    def gather_five(g):
        arrived(blocks_of(g, tensor // 2), ("five", g))

    def wide_weights(which, weight, codes_ref, first_group, last_group):
        @pl.loop(first_group, last_group)
        def _(group):
            for hidden_at in range(hidden_count):
                lanes = pl.ds(hidden_at * BLK, BLK)
                codes = codes_ref[pl.ds(pl.multiple_of(group * 8, 8), 8), lanes]
                scales = take_scales(codes, table_ref)
                for inner in range(4):
                    at = group * 4 + inner
                    rows = pl.ds(pl.multiple_of(at * BLK, BLK), BLK)
                    slot = picks[(which * width_count + at) * hidden_count + hidden_at]
                    base = scale_tile(
                        weight[rows, lanes], scales[2 * inner : 2 * inner + 1],
                        scales[2 * inner + 1 : 2 * inner + 2],
                    )
                    weight[rows, lanes] = add_block(base, deltas[slot])

    def down_base(first_group, last_group):
        @pl.loop(first_group, last_group)
        def _(group):
            for inner in range(4):
                lanes = pl.ds(pl.multiple_of((group * 4 + inner) * BLK, BLK), BLK)
                scales = take_scales(down_codes[:, lanes], table_ref)
                for hidden_at in range(hidden_count):
                    rows = pl.ds(hidden_at * BLK, BLK)
                    down_w[rows, lanes] = scale_tile(
                        down_w[rows, lanes], scales[2 * hidden_at : 2 * hidden_at + 1],
                        scales[2 * hidden_at + 1 : 2 * hidden_at + 2],
                    )

    def down_blocks(first_group, last_group):
        @pl.loop(first_group, last_group)
        def _(group):
            for inner in range(4):
                at = group * 4 + inner
                lanes = pl.ds(pl.multiple_of(at * BLK, BLK), BLK)
                for hidden_at in range(hidden_count):
                    rows = pl.ds(hidden_at * BLK, BLK)
                    slot = picks[(2 * width_count + at) * hidden_count + hidden_at]
                    down_w[rows, lanes] = add_block(down_w[rows, lanes], deltas[slot])

    def across(first, count):
        return jnp.concatenate([held[first + at] for at in range(count)], axis=1)

    def project(weight, into, first_step, last_step):
        if first_step == 0:
            into[...] = jnp.zeros_like(into)

        @pl.loop(first_step, last_step)
        def _(step):
            rows = pl.ds(pl.multiple_of(step * 8 * BLK, BLK), 8 * BLK)
            into[...] += jnp.dot(
                across(step * 8, 8), weight[rows, :], preferred_element_type=jnp.float32
            )

    def activate():
        @pl.loop(0, tokens // BLK)
        def _(chunk):
            rows = pl.ds(pl.multiple_of(chunk * BLK, BLK), BLK)
            for at in range(hidden_count):
                lanes = pl.ds(at * BLK, BLK)
                gate, up = gate_pre[rows, lanes], up_pre[rows, lanes]
                sig = 1.0 / (1.0 + jnp.exp(-gate))
                gated = gate * sig
                held[2 * tensor + at, rows] = (gated * up).astype(jnp.bfloat16)
                gate_pre[rows, lanes] = gated
                up_pre[rows, lanes] = up * sig * (1.0 + gate * (1.0 - sig))

    def back_hidden():
        grad_hidden[...] = jnp.zeros_like(grad_hidden)

        @pl.loop(0, width_count // 8)
        def _(step):
            lanes = pl.ds(pl.multiple_of(step * 8 * BLK, BLK), 8 * BLK)
            grad_hidden[...] += lax.dot_general(
                across(tensor + step * 8, 8), down_w[:, lanes], contract_last,
                preferred_element_type=jnp.float32,
            )

    def back_gates():
        @pl.loop(0, tokens // BLK)
        def _(chunk):
            rows = pl.ds(pl.multiple_of(chunk * BLK, BLK), BLK)
            for at in range(hidden_count):
                lanes = pl.ds(at * BLK, BLK)
                grad = grad_hidden[rows, lanes]
                held[2 * tensor + hidden_count + at, rows] = (grad * up_pre[rows, lanes]).astype(
                    jnp.bfloat16
                )
                held[2 * tensor + 2 * hidden_count + at, rows] = (
                    grad * gate_pre[rows, lanes]
                ).astype(jnp.bfloat16)

    parts, pairs = (out_parts, input_parts), (out_pair, input_pair)

    def share(r, row, col):
        chip = row * SIDE + col
        if r == 0:
            columns = pl.ds(pl.multiple_of(chip * 2 * BLK, 2 * BLK), 2 * BLK)
            return jnp.dot(
                across(2 * tensor, hidden_count), down_w[:, columns],
                preferred_element_type=jnp.float32,
            )
        rows = pl.ds(pl.multiple_of(chip * 2 * BLK, 2 * BLK), 2 * BLK)
        return lax.dot_general(
            across(2 * tensor + hidden_count, 2 * hidden_count),
            jnp.concatenate([gate_w[rows, :], up_w[rows, :]], axis=1), contract_last,
            preferred_element_type=jnp.float32,
        )

    def odd(at):
        return 1 + 2 * lax.rem(at, 2)

    orders = (
        (4, lambda at: (2, at)),
        (3, lambda at: (at + lax.div(at, 2), 2)),
        (4, lambda at: (1 + 2 * lax.div(at, 2), odd(at))),
        (4, lambda at: (odd(at) * (1 - lax.div(at, 2)), odd(at) * lax.div(at, 2))),
        (1, lambda at: (at, at)),
    )

    def make_parts(r, order):
        count, steps = orders[order]
        each = 2 if count % 2 == 0 else count

        def some(first):
            spots = []
            for at in range(each):
                dy, dx = steps(first + at)
                spots.append((lax.rem(y + dy, SIDE), lax.rem(x + dx, SIDE)))
            for row, col in spots:
                both = share(r, row, col).astype(jnp.bfloat16)
                parts[r][row, col, 0] = both[:, :BLK]
                parts[r][row, col, 1] = both[:, BLK:]
            for row, col in spots:
                push(parts[r].at[row, col, other], pairs[r].at[row, col], (z, sibling), ("p", r), ("p", r, order))

        if each == count:
            some(jnp.int32(0))
        else:
            pl.loop(0, count // each)(lambda at: some(at * each))

    def add_pairs(r, order):
        count, steps = orders[order]
        arrived(pairs[r].at[0, pl.ds(0, count)], ("p", r, order))

        @pl.loop(0, count)
        def _(at):
            dy, dx = steps(at)
            row, col = lax.rem(y + dy, SIDE), lax.rem(x + dx, SIDE)
            parts[r][row, col, core] = (
                parts[r][row, col, core].astype(jnp.float32)
                + pairs[r][row, col].astype(jnp.float32)
            ).astype(jnp.bfloat16)

    def cell(r, h, df, dg, piece=None):
        rows = pl.ds(h * half, half) if piece is None else pl.ds(h * half + piece * part, part)
        dy, dx = (df, dg) if h == 0 else (dg, df)
        return parts[r].at[lax.rem(y + dy, SIDE), lax.rem(x + dx, SIDE), core, rows]

    def chip(h, df, dg):
        return (z, spot(df, dg) if h == 0 else spot(dg, df))

    def add_into(target, *terms):
        total = target[...].astype(jnp.float32)
        for term in terms:
            total = total + term[...].astype(jnp.float32)
        target[...] = total.astype(jnp.bfloat16)

    ways = ((0, 1), (1, 3))
    across_order = (2, 1, 3, 0)

    def reduce_one(r):
        for dg in across_order:
            for h in range(2):
                for piece, onward in ways:
                    push(cell(r, h, 2, dg, piece), far_one.at[r, dg, h, piece], chip(h, onward, 0), ("a", r), ("a", r, dg))

    def reduce_two(r, dg):
        arrived(far_one.at[r, dg], ("a", r, dg))
        for h in range(2):
            for piece, onward in ways:
                add_into(cell(r, h, onward, dg, piece), far_one.at[r, dg, h, piece])
                push(cell(r, h, onward, dg), far_all.at[r, dg, h, piece], chip(h, onward, 0), ("b", r), ("b", r, dg))

    def far_sum(r, dg):
        arrived(far_all.at[r, dg], ("b", r, dg))
        for h in range(2):
            add_into(cell(r, h, 0, dg), far_all.at[r, dg, h, 0], far_all.at[r, dg, h, 1])

    def reduce_three(r):
        far_sum(r, 2)
        for h in range(2):
            for piece, onward in ways:
                push(cell(r, h, 0, 2, piece), near_one.at[r, h, piece], chip(h, 0, onward), ("c", r), ("c", r))

    def reduce_four(r):
        far_sum(r, 1)
        far_sum(r, 3)
        arrived(near_one.at[r], ("c", r))
        for h in range(2):
            for piece, onward in ways:
                add_into(cell(r, h, 0, onward, piece), near_one.at[r, h, piece])
                push(cell(r, h, 0, onward), near_all.at[r, h, piece], chip(h, 0, onward), ("d", r), ("d", r))

    def reduce_five(r, result):
        far_sum(r, 0)
        arrived(near_all.at[r], ("d", r))
        for h in range(2):
            result[pl.ds(h * half, half), :] = (
                cell(r, h, 0, 0)[...].astype(jnp.float32)
                + near_all[r, h, 0].astype(jnp.float32)
                + near_all[r, h, 1].astype(jnp.float32)
            ).astype(jnp.bfloat16)

    def block_grads():
        base = 3 * width_count * hidden_count

        @pl.loop(0, groups)
        def _(slot):
            grads[slot] = lax.dot_general(
                held[picks[base + slot]], held[picks[base + groups + slot]], contract_first,
                preferred_element_type=jnp.float32,
            ).astype(jnp.bfloat16)

        for step in range(1, groups):
            to = lax.rem(z + step, groups)
            push(grads.at[to], grads_in.at[step - 1], (to, t), ("h",), ("h",))

    def adam():
        total = grads[z].astype(jnp.float32)
        arrived(grads_in, ("h",))
        for step in range(1, groups):
            total = total + grads_in[step - 1].astype(jnp.float32)
        moment = beta_one * first[0, 0].astype(jnp.float32) + (1.0 - beta_one) * total
        square = (
            beta_two * second[0, 0].astype(jnp.float32) + (1.0 - beta_two) * total * total
        )
        bias_one = 1.0 - beta_one**ADAM_STEP
        bias_two = 1.0 - beta_two**ADAM_STEP
        step_size = learn_rate * (moment / bias_one) / (jnp.sqrt(square / bias_two) + adam_eps)
        new_delta[0, 0] = delta_ref[0, 0] - step_size
        new_first[0, 0] = moment.astype(jnp.bfloat16)
        new_second[0, 0] = square.astype(jnp.bfloat16)

    gather_zero(0)
    spread_own(0)
    for step in range(1, groups):
        push(deltas.at[z], deltas.at[z], (lax.rem(z + step, groups), t), ("w",), ("w",))
    for load in loads[1:4]:
        load.wait()
    down_base(0, 8)
    gather_one(0)
    gather_three(0, 0)
    for load in loads[4:]:
        load.wait()
    gather_two(0)
    arrived(deltas.at[pl.ds(0, groups - 1)], ("w",))
    wide_weights(0, gate_w, gate_codes, 0, 4)
    gather_three(0, 3)
    gather_three(0, 1)
    gather_zero(1)
    wide_weights(0, gate_w, gate_codes, 4, 8)
    gather_four(0, 0)
    gather_three(0, 2)
    spread_own(1)
    wide_weights(1, up_w, up_codes, 0, 4)
    gather_four(0, 3)
    gather_four(0, 1)
    wide_weights(1, up_w, up_codes, 4, 8)
    gather_one(1)
    gather_four(0, 2)
    down_blocks(0, 4)
    gather_three(1, 0)
    gather_five(0)
    project(gate_w, gate_pre, 0, 2)
    gather_two(1)
    project(gate_w, gate_pre, 2, 4)
    project(up_w, up_pre, 0, 2)
    gather_three(1, 3)
    gather_three(1, 1)
    project(up_w, up_pre, 2, 4)
    gather_three(1, 2)
    gather_four(1, 0)
    activate()
    down_blocks(4, 8)
    make_parts(0, 0)
    gather_four(1, 3)
    gather_four(1, 1)
    make_parts(0, 1)
    gather_four(1, 2)
    add_pairs(0, 0)
    add_pairs(0, 1)
    reduce_one(0)
    for order in (2, 3, 4):
        make_parts(0, order)
    gather_five(1)
    back_hidden()
    add_pairs(0, 2)
    for dg in (2, 1, 3):
        reduce_two(0, dg)
    add_pairs(0, 3)
    add_pairs(0, 4)
    reduce_two(0, 0)
    back_gates()
    for order in (0, 1, 2):
        make_parts(1, order)
    reduce_three(0)
    add_pairs(1, 0)
    add_pairs(1, 1)
    reduce_one(1)
    block_grads()
    reduce_four(0)
    make_parts(1, 3)
    make_parts(1, 4)
    add_pairs(1, 2)
    for dg in (2, 1, 3):
        reduce_two(1, dg)
    add_pairs(1, 3)
    add_pairs(1, 4)
    reduce_three(1)
    reduce_two(1, 0)
    reduce_five(0, out_ref)
    reduce_four(1)
    adam()
    reduce_five(1, input_ref)
    left(deltas.at[pl.ds(0, groups - 1)], ("w",))
    left(grads_in, ("h",))
    for r in range(2):
        left(blocks_of(r, tensor - 1), ("g", r))
        left(pairs[r], ("p", r))
        left(far_one.at[r], ("a", r))
        left(far_all.at[r], ("b", r))
        left(near_one.at[r], ("c", r))
        left(near_all.at[r], ("d", r))
    assert len(leaving) <= SENDS and len(landing) <= ARRIVALS, (len(leaving), len(landing))


def hand_over(*refs):
    count = len(refs) // 2
    for at in range(count):
        refs[count + at][...] = refs[at][...]


def slot_picks(pattern, width_count, hidden_count, hidden_first):
    slots = pattern.shape[0]
    matrix, width_at, hidden_at = pattern[:, 0], pattern[:, 1], pattern[:, 2] - hidden_first
    place = (matrix * width_count + width_at) * hidden_count + hidden_at
    tiles = jnp.arange(3 * width_count * hidden_count, dtype=jnp.int32)
    found = jnp.where(
        place[:, None] == tiles[None, :], jnp.arange(slots, dtype=jnp.int32)[:, None], slots
    )
    base = 2 * width_count
    left = jnp.where(matrix == 2, base + hidden_at, width_at)
    right = jnp.where(
        matrix == 2, width_count + width_at, base + (1 + matrix) * hidden_count + hidden_at
    )
    return jnp.concatenate([jnp.min(found, axis=0), left, right])


def local(
    groups,
    activations, cotangent, gate_levels, up_levels, down_levels, gate_scales, up_scales, down_scales,
    scale_table, block_pattern, delta_master, first_moment, second_moment,
):
    tokens = activations.shape[0]
    width, hidden = gate_levels.shape
    width_count, hidden_count = width // BLK, hidden // BLK
    half, part = tokens // 2, tokens // 4
    picks = slot_picks(
        block_pattern[0], width_count, hidden_count, lax.axis_index("tensor") * hidden_count
    )
    vmem = pl.BlockSpec(memory_space=pltpu.VMEM)
    anywhere = pl.BlockSpec(memory_space=pl.ANY)
    narrow, wide = jnp.bfloat16, jnp.float32
    shapes = [
        jax.ShapeDtypeStruct(v.shape, v.dtype)
        for v in (activations, activations, delta_master, first_moment, second_moment)
    ]
    results = pl.pallas_call(
        functools.partial(layer_kernel, groups),
        out_shape=shapes,
        in_specs=[anywhere] * 8 + [vmem]
        + [pl.BlockSpec(memory_space=pltpu.SMEM), vmem, anywhere, anywhere],
        out_specs=[vmem] * 5,
        scratch_shapes=[
            pltpu.VMEM(first_moment.shape, narrow),
            pltpu.VMEM(second_moment.shape, narrow),
            pltpu.VMEM((2 * width_count + 3 * hidden_count, tokens, BLK), narrow),
            pltpu.VMEM((width, hidden), narrow),
            pltpu.VMEM((width, hidden), narrow),
            pltpu.VMEM((hidden, width), narrow),
            pltpu.VMEM(gate_scales.shape, jnp.int32),
            pltpu.VMEM(up_scales.shape, jnp.int32),
            pltpu.VMEM(down_scales.shape, jnp.int32),
            pltpu.VMEM((tokens, hidden), wide),
            pltpu.VMEM((tokens, hidden), wide),
            pltpu.VMEM((tokens, hidden), wide),
            pltpu.VMEM((groups + 1, BLK, BLK), narrow),
            pltpu.VMEM((SIDE, SIDE, CORES, tokens, BLK), narrow),
            pltpu.VMEM((SIDE, SIDE, CORES, tokens, BLK), narrow),
            pltpu.VMEM((SIDE, SIDE, tokens, BLK), narrow),
            pltpu.VMEM((SIDE, SIDE, tokens, BLK), narrow),
            pltpu.VMEM((2, SIDE, 2, 2, part, BLK), narrow),
            pltpu.VMEM((2, SIDE, 2, 2, half, BLK), narrow),
            pltpu.VMEM((2, 2, 2, part, BLK), narrow),
            pltpu.VMEM((2, 2, 2, half, BLK), narrow),
            pltpu.VMEM((groups, BLK, BLK), narrow),
            pltpu.VMEM((groups - 1, BLK, BLK), narrow),
            pltpu.SemaphoreType.DMA((SENDS,)),
            pltpu.SemaphoreType.DMA((ARRIVALS,)),
            pltpu.SemaphoreType.DMA((10,)),
        ],
        compiler_params=pltpu.CompilerParams(
            collective_id=0, has_side_effects=True, vmem_limit_bytes=58 * 1024 * 1024
        ),
        cost_estimate=pl.CostEstimate(
            flops=13_000_000_000, bytes_accessed=14_000_000, transcendentals=262_144
        ),
    )(
        activations, cotangent, gate_levels, up_levels, down_levels, gate_scales, up_scales,
        down_scales, scale_table.reshape(1, 256), picks, delta_master, first_moment, second_moment,
    )
    return pl.pallas_call(
        hand_over,
        out_shape=shapes,
        in_specs=[vmem] * 5,
        out_specs=[vmem] * 5,
    )(*results)


def solution(mesh):
    in_specs = (
        P("dp", "tensor"),
        P("dp", "tensor"),
        P(None, "tensor"),
        P(None, "tensor"),
        P("tensor", None),
        P(None, "tensor"),
        P(None, "tensor"),
        P("tensor", None),
        P(),
        P("tensor", None, None),
        P("tensor", "dp", None, None),
        P("tensor", "dp", None, None),
        P("tensor", "dp", None, None),
    )
    out_specs = (
        P("dp", "tensor"),
        P("dp", "tensor"),
        P("tensor", "dp", None, None),
        P("tensor", "dp", None, None),
        P("tensor", "dp", None, None),
    )
    return jax.shard_map(
        functools.partial(local, mesh.shape["dp"]),
        mesh=mesh, in_specs=in_specs, out_specs=out_specs, check_vma=False,
    )
```

```python
import functools

import jax
import jax.numpy as jnp
from jax import lax
from jax.experimental import pallas as pl
from jax.experimental.pallas import tpu as pltpu
from jax.sharding import PartitionSpec as P

BLK = 128
QBLK = 64
ADAM_STEP = 20
SIDE = 4
CORES = 2
SENDS = 14
ARRIVALS = 54

beta_one = 0.9
beta_two = 0.999
adam_eps = 1e-08
learn_rate = 0.05

MESH = pl.DeviceIdType.MESH
contract_last = (((1,), (1,)), ((), ()))
contract_first = (((0,), (0,)), ((), ()))


def take_scales(codes, table_ref):
    low = jnp.broadcast_to(table_ref[0:1, 0:128], codes.shape)
    high = jnp.broadcast_to(table_ref[0:1, 128:256], codes.shape)
    within = jnp.bitwise_and(codes, 127)
    from_low = jnp.take_along_axis(low, within, axis=1, mode="promise_in_bounds")
    from_high = jnp.take_along_axis(high, within, axis=1, mode="promise_in_bounds")
    return jnp.where(codes < 128, from_low, from_high)


def scale_tile(levels, upper, lower):
    scales = jnp.concatenate(
        [jnp.broadcast_to(upper, (QBLK, BLK)), jnp.broadcast_to(lower, (QBLK, BLK))], axis=0
    )
    return (levels.astype(jnp.float32) * scales).astype(jnp.bfloat16)


def add_block(base, block):
    return (base.astype(jnp.float32) + block.astype(jnp.float32)).astype(jnp.bfloat16)


def layer_kernel(
    groups,
    x_ref, dy_ref, gate_levels, up_levels, down_levels, gate_scales, up_scales, down_scales, table_ref,
    picks, delta_ref, first_ref, second_ref,
    out_ref, input_ref, new_delta, new_first, new_second,
    first, second, held, gate_w, up_w, down_w, gate_codes, up_codes, down_codes, gate_pre, up_pre, grad_hidden, deltas,
    out_parts, input_parts, out_pair, input_pair, far_one, far_all, near_one, near_all,
    grads, grads_in, send_sem, recv_sem, load_sem,
):
    tokens = x_ref.shape[0]
    hidden_count = gate_w.shape[1] // BLK
    width_count = gate_w.shape[0] // BLK
    tensor = width_count
    half, part = tokens // 2, tokens // 4
    z, t = lax.axis_index("dp"), lax.axis_index("tensor")
    core = lax.rem(t, CORES)
    x = lax.rem(lax.div(t, CORES), SIDE)
    y = lax.div(t, CORES * SIDE)

    def spot(dy, dx, which=None):
        row, col = lax.rem(y + dy, SIDE), lax.rem(x + dx, SIDE)
        return (row * SIDE + col) * CORES + (core if which is None else which)

    other = 1 - core
    sibling = spot(0, 0, other)

    leaving, landing = {}, {}

    def copy_of(src, dst, to, send_key, recv_key):
        return pltpu.make_async_remote_copy(
            src_ref=src, dst_ref=dst, send_sem=send_sem.at[leaving.setdefault(send_key, len(leaving))],
            recv_sem=recv_sem.at[landing.setdefault(recv_key, len(landing))],
            device_id=to, device_id_type=MESH,
        )

    def push(src, dst, to, send_key, recv_key):
        copy_of(src, dst, to, send_key, recv_key).start()

    def arrived(like, recv_key):
        pltpu.make_async_remote_copy(
            src_ref=like, dst_ref=like, send_sem=send_sem.at[0],
            recv_sem=recv_sem.at[landing.setdefault(recv_key, len(landing))],
            device_id=(z, sibling), device_id_type=MESH,
        ).wait_recv()

    def left(like, send_key):
        pltpu.make_async_remote_copy(
            src_ref=like, dst_ref=like, send_sem=send_sem.at[leaving[send_key]],
            recv_sem=recv_sem.at[0], device_id=(z, sibling), device_id_type=MESH,
        ).wait_send()

    loads = [
        pltpu.make_async_copy(src, dst, load_sem.at[at])
        for at, (src, dst) in enumerate(
            (
                (x_ref, held.at[t]), (dy_ref, held.at[tensor + t]),
                (down_scales, down_codes), (down_levels, down_w),
                (gate_scales, gate_codes), (gate_levels, gate_w),
                (up_scales, up_codes), (up_levels, up_w),
                (first_ref, first), (second_ref, second),
            )
        )
    ]
    for load in loads:
        load.start()
    barrier = pltpu.get_barrier_semaphore()
    partners = [(z, spot(0, 1)), (z, spot(0, 3)), (z, spot(1, 0)), (z, spot(3, 0)), (z, sibling)]
    partners += [(lax.rem(z + step, groups), t) for step in range(1, groups)]
    for partner in partners:
        pl.semaphore_signal(barrier, inc=1, device_id=partner, device_id_type=MESH)
    deltas[z] = delta_ref[0, 0].astype(jnp.bfloat16)
    deltas[groups] = jnp.zeros((BLK, BLK), jnp.bfloat16)
    loads[0].wait()
    pl.semaphore_wait(barrier, len(partners))

    def block(g, h, dp, ds, piece=None, which=None):
        at = spot(ds, dp, which) if h == 0 else spot(dp, ds, which)
        rows = pl.ds(h * half, half) if piece is None else pl.ds(h * half + piece * part, part)
        return held.at[g * tensor + at, rows]

    def node(h, dp, ds):
        return (z, spot(ds, dp) if h == 0 else spot(dp, ds))

    def spread(g, h, dp):
        whole = block(g, h, dp, 0)
        push(whole, whole, node(h, 0, 1), ("g", g), ("three", g, dp))
        push(whole, whole, node(h, 0, 3), ("g", g), ("three", g, dp))
        push(whole, whole, (z, sibling), ("g", g), ("five", g))

    def blocks_of(g, count):
        return held.at[pl.ds(g * tensor, count)]

    def gather_zero(g):
        for h in range(2):
            whole = block(g, h, 0, 0)
            push(whole, whole, node(h, 1, 0), ("g", g), ("one", g))
            push(whole, whole, node(h, 3, 0), ("g", g), ("one", g))

    def spread_own(g):
        for h in range(2):
            spread(g, h, 0)

    def gather_one(g):
        arrived(blocks_of(g, 2), ("one", g))
        for h in range(2):
            for dp, piece, onward in ((3, 0, 1), (1, 1, 3)):
                quarter = block(g, h, dp, 0, piece)
                push(quarter, quarter, node(h, onward, 0), ("g", g), ("two", g))
        for h in range(2):
            for dp in (3, 1):
                spread(g, h, dp)

    def gather_two(g):
        arrived(blocks_of(g, 1), ("two", g))
        for h in range(2):
            spread(g, h, 2)

    def gather_three(g, dp):
        arrived(blocks_of(g, 2), ("three", g, dp))
        for h in range(2):
            for ds, piece, onward in ((3, 0, 1), (1, 1, 3)):
                quarter = block(g, h, dp, ds, piece)
                push(quarter, quarter, node(h, 0, onward), ("g", g), ("four", g, dp))
        for h in range(2):
            for ds in (3, 1):
                whole = block(g, h, dp, ds)
                push(whole, whole, (z, sibling), ("g", g), ("five", g))

    def gather_four(g, dp):
        arrived(blocks_of(g, 1), ("four", g, dp))
        for h in range(2):
            whole = block(g, h, dp, 2)
            push(whole, whole, (z, sibling), ("g", g), ("five", g))

    def gather_five(g):
        arrived(blocks_of(g, tensor // 2), ("five", g))

    def wide_weights(which, weight, codes_ref, first_group, last_group):
        @pl.loop(first_group, last_group)
        def _(group):
            for hidden_at in range(hidden_count):
                lanes = pl.ds(hidden_at * BLK, BLK)
                codes = codes_ref[pl.ds(pl.multiple_of(group * 8, 8), 8), lanes]
                scales = take_scales(codes, table_ref)
                for inner in range(4):
                    at = group * 4 + inner
                    rows = pl.ds(pl.multiple_of(at * BLK, BLK), BLK)
                    slot = picks[(which * width_count + at) * hidden_count + hidden_at]
                    base = scale_tile(
                        weight[rows, lanes], scales[2 * inner : 2 * inner + 1],
                        scales[2 * inner + 1 : 2 * inner + 2],
                    )
                    weight[rows, lanes] = add_block(base, deltas[slot])

    def down_base(first_group, last_group):
        @pl.loop(first_group, last_group)
        def _(group):
            for inner in range(4):
                lanes = pl.ds(pl.multiple_of((group * 4 + inner) * BLK, BLK), BLK)
                scales = take_scales(down_codes[:, lanes], table_ref)
                for hidden_at in range(hidden_count):
                    rows = pl.ds(hidden_at * BLK, BLK)
                    down_w[rows, lanes] = scale_tile(
                        down_w[rows, lanes], scales[2 * hidden_at : 2 * hidden_at + 1],
                        scales[2 * hidden_at + 1 : 2 * hidden_at + 2],
                    )

    def down_blocks(first_group, last_group):
        @pl.loop(first_group, last_group)
        def _(group):
            for inner in range(4):
                at = group * 4 + inner
                lanes = pl.ds(pl.multiple_of(at * BLK, BLK), BLK)
                for hidden_at in range(hidden_count):
                    rows = pl.ds(hidden_at * BLK, BLK)
                    slot = picks[(2 * width_count + at) * hidden_count + hidden_at]
                    down_w[rows, lanes] = add_block(down_w[rows, lanes], deltas[slot])

    def across(first, count):
        return jnp.concatenate([held[first + at] for at in range(count)], axis=1)

    def project(weight, into, first_step, last_step):
        if first_step == 0:
            into[...] = jnp.zeros_like(into)

        @pl.loop(first_step, last_step)
        def _(step):
            rows = pl.ds(pl.multiple_of(step * 8 * BLK, BLK), 8 * BLK)
            into[...] += jnp.dot(
                across(step * 8, 8), weight[rows, :], preferred_element_type=jnp.float32
            )

    def activate():
        @pl.loop(0, tokens // BLK)
        def _(chunk):
            rows = pl.ds(pl.multiple_of(chunk * BLK, BLK), BLK)
            for at in range(hidden_count):
                lanes = pl.ds(at * BLK, BLK)
                gate, up = gate_pre[rows, lanes], up_pre[rows, lanes]
                sig = 1.0 / (1.0 + jnp.exp(-gate))
                gated = gate * sig
                held[2 * tensor + at, rows] = (gated * up).astype(jnp.bfloat16)
                gate_pre[rows, lanes] = gated
                up_pre[rows, lanes] = up * sig * (1.0 + gate * (1.0 - sig))

    def back_hidden(first_step, last_step):
        if first_step == 0:
            grad_hidden[...] = jnp.zeros_like(grad_hidden)

        @pl.loop(first_step, last_step)
        def _(step):
            lanes = pl.ds(pl.multiple_of(step * 8 * BLK, BLK), 8 * BLK)
            grad_hidden[...] += lax.dot_general(
                across(tensor + step * 8, 8), down_w[:, lanes], contract_last,
                preferred_element_type=jnp.float32,
            )

    def back_gates():
        @pl.loop(0, tokens // BLK)
        def _(chunk):
            rows = pl.ds(pl.multiple_of(chunk * BLK, BLK), BLK)
            for at in range(hidden_count):
                lanes = pl.ds(at * BLK, BLK)
                grad = grad_hidden[rows, lanes]
                held[2 * tensor + hidden_count + at, rows] = (grad * up_pre[rows, lanes]).astype(
                    jnp.bfloat16
                )
                held[2 * tensor + 2 * hidden_count + at, rows] = (
                    grad * gate_pre[rows, lanes]
                ).astype(jnp.bfloat16)

    parts, pairs = (out_parts, input_parts), (out_pair, input_pair)

    def share(r, row, col):
        chip = row * SIDE + col
        if r == 0:
            columns = pl.ds(pl.multiple_of(chip * 2 * BLK, 2 * BLK), 2 * BLK)
            return jnp.dot(
                across(2 * tensor, hidden_count), down_w[:, columns],
                preferred_element_type=jnp.float32,
            )
        rows = pl.ds(pl.multiple_of(chip * 2 * BLK, 2 * BLK), 2 * BLK)
        return lax.dot_general(
            across(2 * tensor + hidden_count, 2 * hidden_count),
            jnp.concatenate([gate_w[rows, :], up_w[rows, :]], axis=1), contract_last,
            preferred_element_type=jnp.float32,
        )

    def odd(at):
        return 1 + 2 * lax.rem(at, 2)

    orders = (
        (4, lambda at: (2, at)),
        (3, lambda at: (at + lax.div(at, 2), 2)),
        (4, lambda at: (1 + 2 * lax.div(at, 2), odd(at))),
        (4, lambda at: (odd(at) * (1 - lax.div(at, 2)), odd(at) * lax.div(at, 2))),
        (1, lambda at: (at, at)),
    )

    def make_parts(r, order):
        count, steps = orders[order]
        each = 2 if count % 2 == 0 else count

        def some(first):
            spots = []
            for at in range(each):
                dy, dx = steps(first + at)
                spots.append((lax.rem(y + dy, SIDE), lax.rem(x + dx, SIDE)))
            for row, col in spots:
                both = share(r, row, col).astype(jnp.bfloat16)
                parts[r][row, col, 0] = both[:, :BLK]
                parts[r][row, col, 1] = both[:, BLK:]
            for row, col in spots:
                push(parts[r].at[row, col, other], pairs[r].at[row, col], (z, sibling), ("p", r), ("p", r, order))

        if each == count:
            some(jnp.int32(0))
        else:
            pl.loop(0, count // each)(lambda at: some(at * each))

    def add_pairs(r, order):
        count, steps = orders[order]
        arrived(pairs[r].at[0, pl.ds(0, count)], ("p", r, order))

        @pl.loop(0, count)
        def _(at):
            dy, dx = steps(at)
            row, col = lax.rem(y + dy, SIDE), lax.rem(x + dx, SIDE)
            parts[r][row, col, core] = (
                parts[r][row, col, core].astype(jnp.float32)
                + pairs[r][row, col].astype(jnp.float32)
            ).astype(jnp.bfloat16)

    def cell(r, h, df, dg, piece=None):
        rows = pl.ds(h * half, half) if piece is None else pl.ds(h * half + piece * part, part)
        dy, dx = (df, dg) if h == 0 else (dg, df)
        return parts[r].at[lax.rem(y + dy, SIDE), lax.rem(x + dx, SIDE), core, rows]

    def chip(h, df, dg):
        return (z, spot(df, dg) if h == 0 else spot(dg, df))

    def add_into(target, *terms):
        total = target[...].astype(jnp.float32)
        for term in terms:
            total = total + term[...].astype(jnp.float32)
        target[...] = total.astype(jnp.bfloat16)

    ways = ((0, 1), (1, 3))
    across_order = (2, 1, 3, 0)

    def reduce_one(r):
        for dg in across_order:
            for h in range(2):
                for piece, onward in ways:
                    push(cell(r, h, 2, dg, piece), far_one.at[r, dg, h, piece], chip(h, onward, 0), ("a", r), ("a", r, dg))

    def reduce_two(r, dg):
        arrived(far_one.at[r, dg], ("a", r, dg))
        for h in range(2):
            for piece, onward in ways:
                add_into(cell(r, h, onward, dg, piece), far_one.at[r, dg, h, piece])
                push(cell(r, h, onward, dg), far_all.at[r, dg, h, piece], chip(h, onward, 0), ("b", r), ("b", r, dg))

    def far_sum(r, dg):
        arrived(far_all.at[r, dg], ("b", r, dg))
        for h in range(2):
            add_into(cell(r, h, 0, dg), far_all.at[r, dg, h, 0], far_all.at[r, dg, h, 1])

    def reduce_three(r):
        far_sum(r, 2)
        for h in range(2):
            for piece, onward in ways:
                push(cell(r, h, 0, 2, piece), near_one.at[r, h, piece], chip(h, 0, onward), ("c", r), ("c", r))

    def reduce_four(r):
        far_sum(r, 1)
        far_sum(r, 3)
        arrived(near_one.at[r], ("c", r))
        for h in range(2):
            for piece, onward in ways:
                add_into(cell(r, h, 0, onward, piece), near_one.at[r, h, piece])
                push(cell(r, h, 0, onward), near_all.at[r, h, piece], chip(h, 0, onward), ("d", r), ("d", r))

    def reduce_five(r, result):
        far_sum(r, 0)
        arrived(near_all.at[r], ("d", r))
        for h in range(2):
            result[pl.ds(h * half, half), :] = (
                cell(r, h, 0, 0)[...].astype(jnp.float32)
                + near_all[r, h, 0].astype(jnp.float32)
                + near_all[r, h, 1].astype(jnp.float32)
            ).astype(jnp.bfloat16)

    def block_grads():
        base = 3 * width_count * hidden_count

        @pl.loop(0, groups)
        def _(slot):
            grads[slot] = lax.dot_general(
                held[picks[base + slot]], held[picks[base + groups + slot]], contract_first,
                preferred_element_type=jnp.float32,
            ).astype(jnp.bfloat16)

        for step in range(1, groups):
            to = lax.rem(z + step, groups)
            push(grads.at[to], grads_in.at[step - 1], (to, t), ("h",), ("h",))

    def adam():
        total = grads[z].astype(jnp.float32)
        arrived(grads_in, ("h",))
        for step in range(1, groups):
            total = total + grads_in[step - 1].astype(jnp.float32)
        moment = beta_one * first[0, 0].astype(jnp.float32) + (1.0 - beta_one) * total
        square = (
            beta_two * second[0, 0].astype(jnp.float32) + (1.0 - beta_two) * total * total
        )
        bias_one = 1.0 - beta_one**ADAM_STEP
        bias_two = 1.0 - beta_two**ADAM_STEP
        step_size = learn_rate * (moment / bias_one) / (jnp.sqrt(square / bias_two) + adam_eps)
        new_delta[0, 0] = delta_ref[0, 0] - step_size
        new_first[0, 0] = moment.astype(jnp.bfloat16)
        new_second[0, 0] = square.astype(jnp.bfloat16)

    gather_zero(0)
    spread_own(0)
    for step in range(1, groups):
        push(deltas.at[z], deltas.at[z], (lax.rem(z + step, groups), t), ("w",), ("w",))
    for load in loads[1:4]:
        load.wait()
    down_base(0, 8)
    gather_one(0)
    gather_three(0, 0)
    for load in loads[4:]:
        load.wait()
    gather_two(0)
    arrived(deltas.at[pl.ds(0, groups - 1)], ("w",))
    wide_weights(0, gate_w, gate_codes, 0, 4)
    gather_three(0, 3)
    gather_three(0, 1)
    gather_zero(1)
    wide_weights(0, gate_w, gate_codes, 4, 8)
    gather_four(0, 0)
    gather_three(0, 2)
    spread_own(1)
    wide_weights(1, up_w, up_codes, 0, 4)
    down_blocks(0, 4)
    gather_four(0, 3)
    gather_four(0, 1)
    wide_weights(1, up_w, up_codes, 4, 8)
    gather_one(1)
    gather_four(0, 2)
    down_blocks(4, 8)
    gather_three(1, 0)
    gather_five(0)
    project(gate_w, gate_pre, 0, 2)
    project(gate_w, gate_pre, 2, 4)
    gather_two(1)
    project(up_w, up_pre, 0, 2)
    gather_three(1, 3)
    gather_three(1, 1)
    project(up_w, up_pre, 2, 4)
    gather_three(1, 2)
    gather_four(1, 0)
    activate()
    make_parts(0, 0)
    make_parts(0, 1)
    add_pairs(0, 0)
    add_pairs(0, 1)
    reduce_one(0)
    gather_four(1, 3)
    gather_four(1, 1)
    make_parts(0, 2)
    gather_four(1, 2)
    make_parts(0, 3)
    make_parts(0, 4)
    gather_five(1)
    back_hidden(0, 2)
    reduce_two(0, 2)
    add_pairs(0, 2)
    reduce_two(0, 1)
    reduce_two(0, 3)
    back_hidden(2, 4)
    add_pairs(0, 3)
    add_pairs(0, 4)
    reduce_two(0, 0)
    back_gates()
    for order in (0, 1, 2):
        make_parts(1, order)
    reduce_three(0)
    add_pairs(1, 0)
    add_pairs(1, 1)
    reduce_one(1)
    block_grads()
    make_parts(1, 3)
    reduce_two(1, 2)
    add_pairs(1, 2)
    reduce_two(1, 1)
    reduce_two(1, 3)
    reduce_four(0)
    make_parts(1, 4)
    reduce_three(1)
    add_pairs(1, 3)
    add_pairs(1, 4)
    reduce_two(1, 0)
    reduce_five(0, out_ref)
    reduce_four(1)
    adam()
    reduce_five(1, input_ref)
    left(deltas.at[pl.ds(0, groups - 1)], ("w",))
    left(grads_in, ("h",))
    for r in range(2):
        left(blocks_of(r, tensor - 1), ("g", r))
        left(pairs[r], ("p", r))
        left(far_one.at[r], ("a", r))
        left(far_all.at[r], ("b", r))
        left(near_one.at[r], ("c", r))
        left(near_all.at[r], ("d", r))
    assert len(leaving) <= SENDS and len(landing) <= ARRIVALS, (len(leaving), len(landing))


def hand_over(*refs):
    count = len(refs) // 2
    for at in range(count):
        refs[count + at][...] = refs[at][...]


def slot_picks(pattern, width_count, hidden_count, hidden_first):
    slots = pattern.shape[0]
    matrix, width_at, hidden_at = pattern[:, 0], pattern[:, 1], pattern[:, 2] - hidden_first
    place = (matrix * width_count + width_at) * hidden_count + hidden_at
    tiles = jnp.arange(3 * width_count * hidden_count, dtype=jnp.int32)
    found = jnp.where(
        place[:, None] == tiles[None, :], jnp.arange(slots, dtype=jnp.int32)[:, None], slots
    )
    base = 2 * width_count
    left = jnp.where(matrix == 2, base + hidden_at, width_at)
    right = jnp.where(
        matrix == 2, width_count + width_at, base + (1 + matrix) * hidden_count + hidden_at
    )
    return jnp.concatenate([jnp.min(found, axis=0), left, right])


def local(
    groups,
    activations, cotangent, gate_levels, up_levels, down_levels, gate_scales, up_scales, down_scales,
    scale_table, block_pattern, delta_master, first_moment, second_moment,
):
    tokens = activations.shape[0]
    width, hidden = gate_levels.shape
    width_count, hidden_count = width // BLK, hidden // BLK
    half, part = tokens // 2, tokens // 4
    picks = slot_picks(
        block_pattern[0], width_count, hidden_count, lax.axis_index("tensor") * hidden_count
    )
    vmem = pl.BlockSpec(memory_space=pltpu.VMEM)
    anywhere = pl.BlockSpec(memory_space=pl.ANY)
    narrow, wide = jnp.bfloat16, jnp.float32
    shapes = [
        jax.ShapeDtypeStruct(v.shape, v.dtype)
        for v in (activations, activations, delta_master, first_moment, second_moment)
    ]
    results = pl.pallas_call(
        functools.partial(layer_kernel, groups),
        out_shape=shapes,
        in_specs=[anywhere] * 8 + [vmem]
        + [pl.BlockSpec(memory_space=pltpu.SMEM), vmem, anywhere, anywhere],
        out_specs=[vmem] * 5,
        scratch_shapes=[
            pltpu.VMEM(first_moment.shape, narrow),
            pltpu.VMEM(second_moment.shape, narrow),
            pltpu.VMEM((2 * width_count + 3 * hidden_count, tokens, BLK), narrow),
            pltpu.VMEM((width, hidden), narrow),
            pltpu.VMEM((width, hidden), narrow),
            pltpu.VMEM((hidden, width), narrow),
            pltpu.VMEM(gate_scales.shape, jnp.int32),
            pltpu.VMEM(up_scales.shape, jnp.int32),
            pltpu.VMEM(down_scales.shape, jnp.int32),
            pltpu.VMEM((tokens, hidden), wide),
            pltpu.VMEM((tokens, hidden), wide),
            pltpu.VMEM((tokens, hidden), wide),
            pltpu.VMEM((groups + 1, BLK, BLK), narrow),
            pltpu.VMEM((SIDE, SIDE, CORES, tokens, BLK), narrow),
            pltpu.VMEM((SIDE, SIDE, CORES, tokens, BLK), narrow),
            pltpu.VMEM((SIDE, SIDE, tokens, BLK), narrow),
            pltpu.VMEM((SIDE, SIDE, tokens, BLK), narrow),
            pltpu.VMEM((2, SIDE, 2, 2, part, BLK), narrow),
            pltpu.VMEM((2, SIDE, 2, 2, half, BLK), narrow),
            pltpu.VMEM((2, 2, 2, part, BLK), narrow),
            pltpu.VMEM((2, 2, 2, half, BLK), narrow),
            pltpu.VMEM((groups, BLK, BLK), narrow),
            pltpu.VMEM((groups - 1, BLK, BLK), narrow),
            pltpu.SemaphoreType.DMA((SENDS,)),
            pltpu.SemaphoreType.DMA((ARRIVALS,)),
            pltpu.SemaphoreType.DMA((10,)),
        ],
        compiler_params=pltpu.CompilerParams(
            collective_id=0, has_side_effects=True, vmem_limit_bytes=58 * 1024 * 1024
        ),
        cost_estimate=pl.CostEstimate(
            flops=13_000_000_000, bytes_accessed=14_000_000, transcendentals=262_144
        ),
    )(
        activations, cotangent, gate_levels, up_levels, down_levels, gate_scales, up_scales,
        down_scales, scale_table.reshape(1, 256), picks, delta_master, first_moment, second_moment,
    )
    return pl.pallas_call(
        hand_over,
        out_shape=shapes,
        in_specs=[vmem] * 5,
        out_specs=[vmem] * 5,
    )(*results)


def solution(mesh):
    in_specs = (
        P("dp", "tensor"),
        P("dp", "tensor"),
        P(None, "tensor"),
        P(None, "tensor"),
        P("tensor", None),
        P(None, "tensor"),
        P(None, "tensor"),
        P("tensor", None),
        P(),
        P("tensor", None, None),
        P("tensor", "dp", None, None),
        P("tensor", "dp", None, None),
        P("tensor", "dp", None, None),
    )
    out_specs = (
        P("dp", "tensor"),
        P("dp", "tensor"),
        P("tensor", "dp", None, None),
        P("tensor", "dp", None, None),
        P("tensor", "dp", None, None),
    )
    return jax.shard_map(
        functools.partial(local, mesh.shape["dp"]),
        mesh=mesh, in_specs=in_specs, out_specs=out_specs, check_vma=False,
    )
```
